512 devices in a mesh: dp: 32 (over x_lo, z), ctx: 16 (over y, x_hi, core).
Axes of the slice: x: 4 (x_hi: 2, x_lo: 2; x = x_hi * 2 + x_lo), y: 4, z: 16, core: 2. Of those that a mesh axis runs over, the one named last changes fastest.
Arguments:
- gate_out: bfloat16 [32, 512, 2048], P('dp', None, 'ctx'), may hold values from -6 to 6
- gate_in: bfloat16 [32, 512, 2048], P('dp', None, 'ctx'), may hold values from -6 to 6
- signal: bfloat16 [32, 512, 2048], P('dp', None, 'ctx'), may hold values from -6 to 6
- cotangent: bfloat16 [32, 512, 2048], P('dp', None, 'ctx'), may hold values from -6 to 6
- residue: float32 [32, 16], replicated, may hold values from -1 to 1
- decay: float32 [32, 16], replicated, may hold values from 0.25 to 64
- skip_bias: float32 [512], replicated, may hold values from -1 to 1
- channel_group: int32 [512], replicated, may hold values from 0 to 31, as said below
Outputs:
- conv_out: bfloat16 [32, 512, 2048], P('dp', None, 'ctx')
- grad_gate_out: bfloat16 [32, 512, 2048], P('dp', None, 'ctx')
- grad_gate_in: bfloat16 [32, 512, 2048], P('dp', None, 'ctx')
- grad_signal: bfloat16 [32, 512, 2048], P('dp', None, 'ctx')
- grad_filter: float32 [32, 2048], P(None, 'ctx')
- grad_residue: float32 [32, 16], replicated
- grad_bias: float32 [512], replicated
The draws below stay inside these ranges and needn't reach their ends.
Inputs may be any that keep to these rules, and one draw needn't show every extreme that they name: `channel_group`: each of the 32 groups is named by exactly 16 channels.
All inputs are finite; a program needn't handle non-finite values.
Results may differ from the reference program's by a relative error of at most 0.01.
Values may be sent and summed in bfloat16 or wider, within the bound.
A program may use at most 64 MiB of HBM per device.

```python
import math
import jax
import jax.numpy as jnp
from jax import lax

GROUP_SIZE = 16
GROUPS = 32
MODES = 16
CHANNELS = 512
SEQ_LEN = 2048
SEQS = 32


def modal_rates(key, slow_share):
    pick = jax.random.uniform(jax.random.fold_in(key, 11), (GROUPS, MODES), jnp.float32)
    spread = jax.random.uniform(jax.random.fold_in(key, 12), (GROUPS, MODES), jnp.float32)
    top_rate = float(max(SEQ_LEN // 32, 4))
    slow_rate = 0.25 * 8.0 ** spread
    fast_rate = 2.0 * (top_rate / 2.0) ** spread
    return jnp.where(pick < slow_share, slow_rate, fast_rate)


def draw_decay(key, part):
    rates = modal_rates(key, 0.5)
    return rates.astype(jnp.float32)


def draw_residue(key, part):
    rates = modal_rates(key, 0.5)
    key = jax.random.fold_in(key, 5)
    noise = jax.random.truncated_normal(key, -4.0, 4.0, (GROUPS, MODES), jnp.float32)
    return (noise * jnp.sqrt(2.0 * rates / (SEQ_LEN * MODES))).astype(jnp.float32)


def draw_channel_group(key, part):
    key = jax.random.fold_in(key, 7)
    order = jax.random.permutation(key, CHANNELS)
    return (order % GROUPS).astype(jnp.int32)


def levels(stream_key, extent, pieces, smallest, top_value):
    gain = 1.0
    for position, shards_of in pieces:
        draws = jax.random.uniform(jax.random.fold_in(jax.random.fold_in(stream_key, 6), position), (shards_of,), jnp.float32, smallest / len(pieces), top_value / len(pieces))
        gain = gain * jnp.repeat(jnp.exp(draws), extent[position] // shards_of).reshape((-1,) + (1,) * (len(extent) - 1 - position))
    return gain


def gaussian(stream_key, extent, width, limit, split=(), dtype=jnp.bfloat16):
    entries = jax.random.normal(stream_key, extent, jnp.float32) * width
    if len(split) > 0:
        entries = levels(stream_key, extent, split, -0.22, 0.18) * entries
    return jnp.clip(entries, min=-limit, max=limit).astype(dtype)


def setup_inputs(seed: int = 0) -> dict:
    key_of = jax.random.split(jax.random.key(seed), 9)
    gate_out = gaussian(key_of[0], (SEQS, CHANNELS, SEQ_LEN), 1.0, 6.0, ((0, 32), (2, 16)))
    gate_in = gaussian(key_of[1], (SEQS, CHANNELS, SEQ_LEN), 1.0, 6.0, ((0, 32), (2, 16)))
    signal = gaussian(key_of[2], (SEQS, CHANNELS, SEQ_LEN), 1.0, 6.0, ((0, 32), (2, 16)))
    cotangent = gaussian(key_of[3], (SEQS, CHANNELS, SEQ_LEN), 1.0, 6.0, ((0, 32), (2, 16)))
    residue = draw_residue(jax.random.fold_in(key_of[8], 71), 0)
    decay = draw_decay(jax.random.fold_in(key_of[8], 71), 0)
    skip_bias = jnp.clip(jax.random.uniform(key_of[6], (CHANNELS,), jnp.float32, -1.0, 1.0), -1.0, 1.0)
    channel_group = draw_channel_group(jax.random.fold_in(key_of[8], 71), 0)
    return {"gate_out": gate_out, "gate_in": gate_in, "signal": signal, "cotangent": cotangent, "residue": residue, "decay": decay, "skip_bias": skip_bias, "channel_group": channel_group}


def reference(gate_out, gate_in, signal, cotangent, residue, decay, skip_bias, channel_group):
    sequences, channels, seq_len = gate_out.shape
    groups = residue.shape[0]
    doubled = 2 * seq_len
    positions = jnp.arange(seq_len).astype(jnp.float32) / seq_len
    basis = jnp.exp(-decay[:, :, None] * positions[None, None, :])
    filters = jnp.einsum('gm,gmt->gt', residue, basis, precision=lax.Precision.HIGHEST)
    member = (channel_group[:, None] == jnp.arange(groups).astype(jnp.int32)[None, :]).astype(jnp.float32)
    channel_filter = jnp.dot(member, filters, precision=lax.Precision.HIGHEST)
    filter_spec = jnp.fft.rfft(channel_filter, n=doubled, axis=-1)

    def per_sequence(carry, inputs):
        filter_total, bias_total = carry
        gate_row, input_row, signal_row, cotan_row = inputs
        mixed_in = (input_row.astype(jnp.float32) * signal_row.astype(jnp.float32)).astype(jnp.bfloat16)
        back_grad = (cotan_row.astype(jnp.float32) * gate_row.astype(jnp.float32)).astype(jnp.bfloat16)
        mixed_wide = mixed_in.astype(jnp.float32)
        back_wide = back_grad.astype(jnp.float32)
        mixed_spec = jnp.fft.rfft(mixed_wide, n=doubled, axis=-1)
        back_spec = jnp.fft.rfft(back_wide, n=doubled, axis=-1)
        conv_state = jnp.fft.irfft(filter_spec * mixed_spec, n=doubled, axis=-1)[:, :seq_len].astype(jnp.bfloat16)
        conv_back = jnp.fft.irfft(jnp.conj(filter_spec) * back_spec, n=doubled, axis=-1)[:, :seq_len].astype(jnp.bfloat16)
        lagged = jnp.fft.irfft(jnp.conj(mixed_spec) * back_spec, n=doubled, axis=-1)[:, :seq_len]
        mixture = conv_state.astype(jnp.float32) + skip_bias[:, None] * mixed_wide
        conv_out = (gate_row.astype(jnp.float32) * mixture).astype(jnp.bfloat16)
        grad_gate_out = (cotan_row.astype(jnp.float32) * mixture).astype(jnp.bfloat16)
        grad_mixed = conv_back.astype(jnp.float32) + skip_bias[:, None] * back_wide
        grad_gate_in = (grad_mixed * signal_row.astype(jnp.float32)).astype(jnp.bfloat16)
        grad_signal = (grad_mixed * input_row.astype(jnp.float32)).astype(jnp.bfloat16)
        carry = (filter_total + lagged, bias_total + lax.optimization_barrier(jnp.sum(back_wide * mixed_wide, axis=1)))
        return (carry, (conv_out, grad_gate_out, grad_gate_in, grad_signal))
    start = (jnp.zeros((channels, seq_len), jnp.float32), jnp.zeros((channels,), jnp.float32))
    totals, results = lax.scan(per_sequence, start, (gate_out, gate_in, signal, cotangent))
    filter_total, bias_total = totals
    conv_out, grad_gate_out, grad_gate_in, grad_signal = results
    grad_filter = jnp.dot(member.T, filter_total, precision=lax.Precision.HIGHEST) / math.sqrt(sequences * seq_len * GROUP_SIZE)
    grad_residue = jnp.einsum('gt,gmt->gm', grad_filter, basis, precision=lax.Precision.HIGHEST) / math.sqrt(seq_len)
    grad_bias = bias_total / math.sqrt(sequences * seq_len)
    return (conv_out, grad_gate_out, grad_gate_in, grad_signal, grad_filter, grad_residue, grad_bias)
```

```python
import functools
import math

import jax
import jax.numpy as jnp
from jax import lax
from jax.experimental import pallas as pl
from jax.experimental.pallas import tpu as pltpu
from jax.sharding import PartitionSpec as P

GROUP_SIZE = 16
MESH = pl.DeviceIdType.MESH
EXACT = lax.Precision.HIGHEST
F32 = jnp.float32
BF16 = jnp.bfloat16


def iota(shape, dim):
    return lax.broadcasted_iota(jnp.int32, shape, dim)


def matmul(left, right, dims=(1, 0), precision=None):
    return lax.dot_general(
        left,
        right,
        (((dims[0],), (dims[1],)), ((), ())),
        precision=precision,
        preferred_element_type=F32,
    )


def kernel(
    data_size,
    ctx_size,
    gate_out,
    gate_in,
    signal,
    cotangent,
    residue,
    decay,
    skip_bias,
    channel_group,
    conv_out,
    grad_gate_out,
    grad_gate_in,
    grad_signal,
    grad_filter,
    grad_residue,
    grad_bias,
    sorted_in,
    got,
    unsort,
    bias_wide,
    ranks,
    basis,
    taps,
    lags,
    corr_send,
    corr_got,
    back_send,
    back_got,
    sum_got,
    sum_send,
    all_got,
    final,
    send_sems,
    recv_sems,
):
    groups = residue.shape[0]
    channels, rows = gate_out.shape
    seq_len = rows * ctx_size
    own = channels // ctx_size
    own_groups = own // GROUP_SIZE
    share = groups // data_size
    data_index = lax.axis_index("dp")
    ctx_index = lax.axis_index("ctx")

    def over_ctx(step):
        lax.fori_loop(1, ctx_size, lambda o, c: (step(lax.rem(ctx_index + o, ctx_size)), c)[1], 0)

    def over_data(step):
        lax.fori_loop(1, data_size, lambda o, c: (step(lax.rem(data_index + o, data_size)), c)[1], 0)

    def push(src, dst, phase, target):
        pltpu.make_async_remote_copy(
            src_ref=src,
            dst_ref=dst,
            send_sem=send_sems.at[phase],
            recv_sem=recv_sems.at[phase],
            device_id=target,
            device_id_type=MESH,
        ).start()

    def arrived(span, phase):
        pltpu.make_async_copy(span, span, recv_sems.at[phase]).wait()

    def sent(span, phase):
        pltpu.make_async_copy(span, span, send_sems.at[phase]).wait()

    barrier = pltpu.get_barrier_semaphore()
    over_ctx(
        lambda t: pl.semaphore_signal(barrier, inc=1, device_id={"ctx": t}, device_id_type=MESH)
    )
    over_data(
        lambda t: pl.semaphore_signal(barrier, inc=1, device_id={"dp": t}, device_id_type=MESH)
    )

    member = iota((groups, channels), 0) == channel_group[...]
    before = jnp.where(iota((channels, channels), 0) < iota((channels, channels), 1), 1.0, 0.0)
    rank = matmul(jnp.where(member, 1.0, 0.0).astype(BF16), before.astype(BF16))
    rank = jnp.sum(jnp.where(member, rank, 0.0), axis=0, keepdims=True)
    ranks[...] = rank
    first = jnp.sum(
        jnp.where(member, iota((groups, channels), 0).astype(F32), 0.0), axis=0, keepdims=True
    )
    place = first * GROUP_SIZE + rank
    sort = jnp.where(iota((channels, channels), 0).astype(F32) == place, 1.0, 0.0).astype(BF16)

    mixed = (gate_in[...].astype(F32) * signal[...].astype(F32)).astype(BF16)
    back = (cotangent[...].astype(F32) * gate_out[...].astype(F32)).astype(BF16)
    sorted_in[...] = matmul(sort, jnp.concatenate([mixed, back], axis=1)).astype(BF16)
    got[ctx_index] = sorted_in[pl.ds(pl.multiple_of(ctx_index * own, own), own)]

    pl.semaphore_wait(barrier, ctx_size - 1 + data_size - 1)
    over_ctx(
        lambda t: push(
            sorted_in.at[pl.ds(pl.multiple_of(t * own, own), own)],
            got.at[ctx_index],
            0,
            {"ctx": t},
        )
    )

    place_wide = jnp.transpose(jnp.broadcast_to(place, (128, channels)))
    unsort[...] = jnp.where(
        iota((channels, channels), 1).astype(F32) == place_wide[:, :1], 1.0, 0.0
    ).astype(BF16)
    bias_wide[...] = jnp.transpose(jnp.broadcast_to(skip_bias[...], (rows, channels)))
    modes = residue.shape[1]
    lane = iota((modes, rows), 1).astype(F32)
    for g in range(own_groups):
        pick = jnp.where(iota((groups, rows), 0) == ctx_index * own_groups + g, 1.0, 0.0)
        rate = matmul(decay[...], pick, (0, 0), EXACT)
        weight = matmul(residue[...], pick, (0, 0), EXACT)
        for i in range(ctx_size):
            basis[g, :, i * rows : (i + 1) * rows] = jnp.exp(-rate * ((lane + i * rows) / seq_len))
        filt = matmul(weight * jnp.exp(rate * (lane / seq_len)), basis[g], (0, 0), EXACT)
        causal = iota((rows, rows), 1) >= iota((rows, rows), 0)
        taps[g, :, :rows] = jnp.zeros((rows, rows), BF16)
        taps[g, :, rows : 2 * rows] = jnp.where(causal, filt[:, :rows], 0.0).astype(BF16)
        taps[g, :, 2 * rows :] = filt[:, rows:].astype(BF16)

    arrived(got.at[pl.ds(0, ctx_size - 1)], 0)

    for g in range(own_groups):
        mine = slice(g * GROUP_SIZE, (g + 1) * GROUP_SIZE)
        blocks = ctx_size * GROUP_SIZE
        mix = got[:, mine, :rows].reshape(blocks, rows)
        grad = got[:, mine, rows:].reshape(blocks, rows)
        mix_t = jnp.transpose(mix)

        def shifted(k):
            if k == 0:
                return grad
            return jnp.concatenate(
                [grad[k * GROUP_SIZE :], jnp.zeros((k * GROUP_SIZE, rows), BF16)], axis=0
            )

        for k in range(0, ctx_size, 2):
            pair = jnp.concatenate([shifted(k), shifted(k + 1)], axis=1)
            lags[:, k * rows : (k + 2) * rows] = matmul(mix_t, pair)
        lags[:, seq_len:] = jnp.zeros((rows, rows), F32)
        width = seq_len + rows
        parts = [lags[a * 8 : (a + 1) * 8, :] for a in range(rows // 8)]
        shift = 8
        while len(parts) > 1:
            parts = [
                parts[a] + pltpu.roll(parts[a + 1], width - shift, 1)
                for a in range(0, len(parts), 2)
            ]
            shift *= 2
        skew = parts[0]
        row = iota((8, width), 0)
        for bit in (1, 2, 4):
            skew = jnp.where(row & bit != 0, pltpu.roll(skew, width - bit, 1), skew)
        corr = jnp.sum(skew, axis=0, keepdims=True)
        modal = jnp.zeros((modes, rows), F32)
        for i in range(ctx_size):
            span = slice(i * rows, (i + 1) * rows)
            modal = modal + basis[g, :, span] * corr[:, span]
            corr_send[i, g, :, :rows] = corr[:, span]
        direct = jnp.zeros((GROUP_SIZE, rows), F32)
        for i in range(ctx_size):
            direct = direct + got[i, mine, :rows].astype(F32) * got[i, mine, rows:].astype(F32)
        stack = jnp.concatenate(
            [modal, direct, jnp.zeros((rows - modes - GROUP_SIZE, rows), F32)], axis=0
        )
        small = matmul(jnp.ones((8, rows), F32), stack, (1, 1), EXACT)[:1]
        for i in range(ctx_size):
            corr_send[i, g, :, rows:] = small
    for g in range(own_groups):
        corr_got[ctx_index * own_groups + g] = corr_send[ctx_index, g]
    over_ctx(
        lambda t: push(
            corr_send.at[t],
            corr_got.at[pl.ds(ctx_index * own_groups, own_groups)],
            1,
            {"ctx": t},
        )
    )

    pairs = ctx_size // 2
    for g in range(own_groups):
        mine = slice(g * GROUP_SIZE, (g + 1) * GROUP_SIZE)
        wide = [
            jnp.concatenate([got[2 * p, mine, :], got[2 * p + 1, mine, :]], axis=1)
            for p in range(pairs)
        ]
        wide = jnp.concatenate(wide, axis=0)
        mix = jnp.concatenate([wide[:, :rows], wide[:, 2 * rows : 3 * rows]], axis=1)
        grad = jnp.concatenate([wide[:, rows : 2 * rows], wide[:, 3 * rows :]], axis=1)
        state = jnp.zeros((pairs * GROUP_SIZE, 2 * rows), F32)
        prior = jnp.zeros((pairs * GROUP_SIZE, 2 * rows), F32)
        for q in range(pairs):
            block = jnp.concatenate(
                [
                    taps[g, :, (2 * q + 1) * rows : (2 * q + 3) * rows],
                    taps[g, :, 2 * q * rows : (2 * q + 2) * rows],
                ],
                axis=0,
            )
            cut = q * GROUP_SIZE
            left = pairs * GROUP_SIZE - cut
            ahead = matmul(mix[:left], block)
            behind = matmul(grad[cut:], block, (1, 1))
            if q == 0:
                state, prior = ahead, behind
            else:
                gap = jnp.zeros((cut, 2 * rows), F32)
                state = state + jnp.concatenate([gap, ahead], axis=0)
                prior = prior + jnp.concatenate([behind, gap], axis=0)
        state = state.astype(BF16)
        prior = prior.astype(BF16)
        for i in range(ctx_size):
            at = slice((i // 2) * GROUP_SIZE, (i // 2 + 1) * GROUP_SIZE)
            span = slice((i % 2) * rows, (i % 2 + 1) * rows)
            back_send[i, mine, :rows] = state[at, span]
            back_send[i, mine, rows:] = prior[at, span]
    back_got[pl.ds(pl.multiple_of(ctx_index * own, own), own)] = back_send[ctx_index]
    over_ctx(
        lambda t: push(
            back_send.at[t],
            back_got.at[pl.ds(pl.multiple_of(ctx_index * own, own), own)],
            2,
            {"ctx": t},
        )
    )

    arrived(corr_got.at[pl.ds(0, own_groups * (ctx_size - 1))], 1)
    sum_got[data_index] = corr_got[pl.ds(data_index * share, share)]
    over_data(
        lambda t: push(
            corr_got.at[pl.ds(t * share, share)], sum_got.at[data_index], 3, {"dp": t}
        )
    )

    arrived(back_got.at[pl.ds(0, own * (ctx_size - 1))], 2)
    results = matmul(unsort[...], back_got[...])
    wide_gate = gate_out[...].astype(F32)
    wide_cot = cotangent[...].astype(F32)
    wide_in = gate_in[...].astype(F32)
    wide_signal = signal[...].astype(F32)
    mixed_wide = (wide_in * wide_signal).astype(BF16).astype(F32)
    back_wide = (wide_cot * wide_gate).astype(BF16).astype(F32)
    mixture = results[:, :rows] + bias_wide[...] * mixed_wide
    conv_out[...] = (wide_gate * mixture).astype(BF16)
    grad_gate_out[...] = (wide_cot * mixture).astype(BF16)
    grad_mixed = results[:, rows:] + bias_wide[...] * back_wide
    grad_gate_in[...] = (grad_mixed * wide_signal).astype(BF16)
    grad_signal[...] = (grad_mixed * wide_in).astype(BF16)

    arrived(sum_got.at[pl.ds(0, data_size - 1)], 3)
    total = sum_got[0]
    for i in range(1, data_size):
        total = total + sum_got[i]
    at = iota((1, 1, 2 * rows), 2)
    filter_scale = 1.0 / math.sqrt(data_size * seq_len * GROUP_SIZE)
    scale = jnp.where(
        at < rows,
        filter_scale,
        jnp.where(
            at < rows + modes,
            filter_scale / math.sqrt(seq_len),
            1.0 / math.sqrt(data_size * seq_len),
        ),
    )
    sum_send[...] = total * scale
    all_got[pl.ds(data_index * share, share)] = sum_send[...]
    over_data(
        lambda t: push(sum_send, all_got.at[pl.ds(data_index * share, share)], 4, {"dp": t})
    )
    arrived(all_got.at[pl.ds(0, share * (data_size - 1))], 4)
    for g in range(groups):
        final[g : g + 1, :] = all_got[g]
    grad_filter[...] = final[:, :rows]
    small = final[:, rows:]
    grad_residue[...] = small[:, :modes]
    spread = matmul(small, jnp.where(member, 1.0, 0.0), (0, 0), EXACT)
    hit = iota((rows, channels), 0).astype(F32) == ranks[...] + modes
    grad_bias[...] = jnp.sum(jnp.where(hit, spread, 0.0), axis=0, keepdims=True)

    sent(got.at[pl.ds(0, ctx_size - 1)], 0)
    sent(corr_got.at[pl.ds(0, own_groups * (ctx_size - 1))], 1)
    sent(back_got.at[pl.ds(0, own * (ctx_size - 1))], 2)
    sent(sum_got.at[pl.ds(0, data_size - 1)], 3)
    sent(all_got.at[pl.ds(0, share * (data_size - 1))], 4)


def body(gate_out, gate_in, signal, cotangent, residue, decay, skip_bias, channel_group):
    data_size = lax.axis_size("dp")
    ctx_size = lax.axis_size("ctx")
    _, channels, rows = gate_out.shape
    groups, modes = residue.shape
    own = channels // ctx_size
    own_groups = own // GROUP_SIZE
    share = groups // data_size
    seq_len = rows * ctx_size
    vmem = pl.BlockSpec(memory_space=pltpu.VMEM)
    wide = jax.ShapeDtypeStruct((channels, rows), BF16)
    flat = lambda a: a.reshape(channels, rows)
    results = pl.pallas_call(
        functools.partial(kernel, data_size, ctx_size),
        out_shape=[
            wide,
            wide,
            wide,
            wide,
            jax.ShapeDtypeStruct((groups, rows), F32),
            jax.ShapeDtypeStruct((groups, modes), F32),
            jax.ShapeDtypeStruct((1, channels), F32),
        ],
        in_specs=[vmem] * 8,
        out_specs=[vmem] * 7,
        scratch_shapes=[
            pltpu.VMEM((channels, 2 * rows), BF16),
            pltpu.VMEM((ctx_size, own, 2 * rows), BF16),
            pltpu.VMEM((channels, channels), BF16),
            pltpu.VMEM((channels, rows), F32),
            pltpu.VMEM((1, channels), F32),
            pltpu.VMEM((own_groups, modes, seq_len), F32),
            pltpu.VMEM((own_groups, rows, seq_len + rows), BF16),
            pltpu.VMEM((rows, seq_len + rows), F32),
            pltpu.VMEM((ctx_size, own_groups, 1, 2 * rows), F32),
            pltpu.VMEM((groups, 1, 2 * rows), F32),
            pltpu.VMEM((ctx_size, own, 2 * rows), BF16),
            pltpu.VMEM((channels, 2 * rows), BF16),
            pltpu.VMEM((data_size, share, 1, 2 * rows), F32),
            pltpu.VMEM((share, 1, 2 * rows), F32),
            pltpu.VMEM((groups, 1, 2 * rows), F32),
            pltpu.VMEM((groups, 2 * rows), F32),
            pltpu.SemaphoreType.DMA((5,)),
            pltpu.SemaphoreType.DMA((5,)),
        ],
        compiler_params=pltpu.CompilerParams(
            collective_id=0, has_side_effects=True, vmem_limit_bytes=32 * 1024 * 1024
        ),
        cost_estimate=pl.CostEstimate(
            flops=2 * 400_000_000, bytes_accessed=2_000_000, transcendentals=100_000
        ),
    )(
        flat(gate_out),
        flat(gate_in),
        flat(signal),
        flat(cotangent),
        residue,
        decay,
        skip_bias.reshape(1, channels),
        channel_group.reshape(1, channels),
    )
    lifted = tuple(a.reshape(1, channels, rows) for a in results[:4])
    return lifted + (results[4], results[5], results[6].reshape(channels))


def solution(mesh):
    return jax.shard_map(
        body,
        mesh=mesh,
        in_specs=(
            P("dp", None, "ctx"),
            P("dp", None, "ctx"),
            P("dp", None, "ctx"),
            P("dp", None, "ctx"),
            P(),
            P(),
            P(),
            P(),
        ),
        out_specs=(
            P("dp", None, "ctx"),
            P("dp", None, "ctx"),
            P("dp", None, "ctx"),
            P("dp", None, "ctx"),
            P(None, "ctx"),
            P(),
            P(),
        ),
        check_vma=False,
    )
```

```python
import functools
import math

import jax
import jax.numpy as jnp
from jax import lax
from jax.experimental import pallas as pl
from jax.experimental.pallas import tpu as pltpu
from jax.sharding import PartitionSpec as P

GROUP_SIZE = 16
PLANE_SEQS = 2
MESH = pl.DeviceIdType.MESH
EXACT = lax.Precision.HIGHEST
F32 = jnp.float32
BF16 = jnp.bfloat16


def iota(shape, dim):
    return lax.broadcasted_iota(jnp.int32, shape, dim)


def matmul(left, right, dims=(1, 0), precision=None):
    return lax.dot_general(
        left,
        right,
        (((dims[0],), (dims[1],)), ((), ())),
        precision=precision,
        preferred_element_type=F32,
    )


def kernel(
    data_size,
    ctx_size,
    gate_out_hbm,
    gate_in_hbm,
    signal_hbm,
    cotangent_hbm,
    residue_hbm,
    decay_hbm,
    skip_bias_hbm,
    channel_group_hbm,
    conv_out_hbm,
    grad_gate_out_hbm,
    grad_gate_in_hbm,
    grad_signal_hbm,
    grad_filter_hbm,
    grad_residue_hbm,
    grad_bias_hbm,
    gate_out,
    gate_in,
    signal,
    cotangent,
    residue,
    decay,
    skip_bias,
    channel_group,
    load_sems,
    conv_out,
    grad_gate_out,
    grad_gate_in,
    grad_signal,
    grad_filter,
    grad_residue,
    grad_bias,
    store_sems,
    sorted_in,
    got,
    unsort,
    bias_wide,
    ranks,
    basis,
    taps,
    lags,
    term_send,
    term_got,
    back_send,
    back_got,
    sum_send,
    sum_got,
    final,
    send_sems,
    recv_sems,
):
    modes, groups = residue.shape
    channels, rows = gate_out.shape
    seq_len = rows * ctx_size
    depth = data_size // PLANE_SEQS
    blocks = ctx_size * GROUP_SIZE
    ctx_index = lax.axis_index("ctx")
    plane_seq = lax.axis_index("dp") // depth
    level = lax.axis_index("dp") % depth
    plane_index = plane_seq * ctx_size + ctx_index

    def over_plane(step):
        def one(o, c):
            peer = lax.rem(plane_index + o, groups)
            seq = peer // ctx_size
            rank = peer - seq * ctx_size
            step(peer, seq, rank, {"dp": seq * depth + level, "ctx": rank})
            return c

        lax.fori_loop(1, groups, one, 0)

    def over_column(step):
        def one(o, c):
            peer = lax.rem(level + o, depth)
            step({"dp": plane_seq * depth + peer})
            return c

        lax.fori_loop(1, depth, one, 0)

    def push(src, dst, phase, target):
        pltpu.make_async_remote_copy(
            src_ref=src,
            dst_ref=dst,
            send_sem=send_sems.at[phase],
            recv_sem=recv_sems.at[phase],
            device_id=target,
            device_id_type=MESH,
        ).start()

    def arrived(span, phase):
        pltpu.make_async_copy(span, span, recv_sems.at[phase]).wait()

    def sent(span, phase):
        pltpu.make_async_copy(span, span, send_sems.at[phase]).wait()

    def arrived_plane(phase):
        span = sorted_in.at[pl.ds(0, channels - GROUP_SIZE)]
        arrived(span, phase)

    loads = [
        pltpu.make_async_copy(src, dst, load_sems.at[i])
        for i, (src, dst) in enumerate(
            [
                (channel_group_hbm, channel_group),
                (gate_in_hbm, gate_in),
                (signal_hbm, signal),
                (gate_out_hbm, gate_out),
                (cotangent_hbm, cotangent),
                (decay_hbm, decay),
                (residue_hbm, residue),
                (skip_bias_hbm, skip_bias),
            ]
        )
    ]
    for load in loads:
        load.start()
    stores = [
        pltpu.make_async_copy(src, dst, store_sems.at[i])
        for i, (src, dst) in enumerate(
            [
                (conv_out, conv_out_hbm),
                (grad_gate_out, grad_gate_out_hbm),
                (grad_gate_in, grad_gate_in_hbm),
                (grad_signal, grad_signal_hbm),
                (grad_filter, grad_filter_hbm),
                (grad_residue, grad_residue_hbm),
                (grad_bias, grad_bias_hbm),
            ]
        )
    ]

    barrier = pltpu.get_barrier_semaphore()
    over_plane(
        lambda p, s, k, target: pl.semaphore_signal(
            barrier, inc=1, device_id=target, device_id_type=MESH
        )
    )
    over_column(
        lambda target: pl.semaphore_signal(barrier, inc=1, device_id=target, device_id_type=MESH)
    )

    loads[0].wait()
    member = iota((groups, channels), 0) == channel_group[...]
    before = jnp.where(iota((channels, channels), 0) < iota((channels, channels), 1), 1.0, 0.0)
    rank = matmul(jnp.where(member, 1.0, 0.0).astype(BF16), before.astype(BF16))
    rank = jnp.sum(jnp.where(member, rank, 0.0), axis=0, keepdims=True)
    ranks[...] = rank
    first = jnp.sum(
        jnp.where(member, iota((groups, channels), 0).astype(F32), 0.0), axis=0, keepdims=True
    )
    place = first * GROUP_SIZE + rank
    sort = jnp.where(iota((channels, channels), 0).astype(F32) == place, 1.0, 0.0).astype(BF16)

    for load in loads[1:5]:
        load.wait()
    mixed = (gate_in[...].astype(F32) * signal[...].astype(F32)).astype(BF16)
    back = (cotangent[...].astype(F32) * gate_out[...].astype(F32)).astype(BF16)
    sorted_in[...] = matmul(sort, jnp.concatenate([mixed, back], axis=1)).astype(BF16)

    def channels_of(peer):
        return pl.ds(pl.multiple_of(peer * GROUP_SIZE, GROUP_SIZE), GROUP_SIZE)

    got[plane_seq, ctx_index] = sorted_in[channels_of(plane_index)]

    pl.semaphore_wait(barrier, groups - 1 + depth - 1)
    over_plane(
        lambda p, s, k, target: push(
            sorted_in.at[channels_of(p)], got.at[plane_seq, ctx_index], 0, target
        )
    )

    for load in loads[5:]:
        load.wait()
    place_wide = jnp.transpose(jnp.broadcast_to(place, (128, channels)))
    unsort[...] = jnp.where(
        iota((channels, channels), 1).astype(F32) == place_wide[:, :1], 1.0, 0.0
    ).astype(BF16)
    bias_wide[...] = jnp.transpose(jnp.broadcast_to(skip_bias[...], (rows, channels)))
    lane = iota((modes, rows), 1).astype(F32)
    pick = jnp.where(iota((groups, rows), 0) == plane_index, 1.0, 0.0)
    rate = matmul(decay[...], pick, precision=EXACT)
    weight = matmul(residue[...], pick, precision=EXACT)
    for i in range(ctx_size):
        basis[:, i * rows : (i + 1) * rows] = jnp.exp(-rate * ((lane + i * rows) / seq_len))
    filt = matmul(weight * jnp.exp(rate * (lane / seq_len)), basis[...], (0, 0), EXACT)
    causal = iota((rows, rows), 1) >= iota((rows, rows), 0)
    taps[:, :rows] = jnp.zeros((rows, rows), BF16)
    taps[:, rows : 2 * rows] = jnp.where(causal, filt[:, :rows], 0.0).astype(BF16)
    taps[:, 2 * rows :] = filt[:, rows:].astype(BF16)

    arrived_plane(0)

    mixes = [got[s, :, :, :rows].reshape(blocks, rows) for s in range(PLANE_SEQS)]
    grads = [got[s, :, :, rows:].reshape(blocks, rows) for s in range(PLANE_SEQS)]
    mix_t = jnp.transpose(jnp.concatenate(mixes, axis=0))

    def shifted(k):
        if k == 0:
            return jnp.concatenate(grads, axis=0)
        gap = jnp.zeros((k * GROUP_SIZE, rows), BF16)
        return jnp.concatenate([x for a in grads for x in (a[k * GROUP_SIZE :], gap)], axis=0)

    for k in range(0, ctx_size, 2):
        pair = jnp.concatenate([shifted(k), shifted(k + 1)], axis=1)
        lags[:, k * rows : (k + 2) * rows] = matmul(mix_t, pair)
    width = seq_len + rows
    lags[:, seq_len:] = jnp.zeros((rows, rows), F32)
    parts = [lags[a * 8 : (a + 1) * 8, :] for a in range(rows // 8)]
    shift = 8
    while len(parts) > 1:
        parts = [
            parts[a] + pltpu.roll(parts[a + 1], width - shift, 1) for a in range(0, len(parts), 2)
        ]
        shift *= 2
    skew = parts[0]
    row = iota((8, width), 0)
    for bit in (1, 2, 4):
        skew = jnp.where(row & bit != 0, pltpu.roll(skew, width - bit, 1), skew)
    corr = jnp.sum(skew, axis=0, keepdims=True)
    modal = jnp.zeros((modes, rows), F32)
    direct = jnp.zeros((GROUP_SIZE, rows), F32)
    for i in range(ctx_size):
        span = slice(i * rows, (i + 1) * rows)
        modal = modal + basis[:, span] * corr[:, span]
        for s in range(PLANE_SEQS):
            direct = direct + got[s, i, :, :rows].astype(F32) * got[s, i, :, rows:].astype(F32)
    stack = jnp.concatenate(
        [modal, direct, jnp.zeros((rows - modes - GROUP_SIZE, rows), F32)], axis=0
    )
    term_send[:, :seq_len] = corr[:, :seq_len]
    term_send[:, seq_len:] = matmul(jnp.ones((8, rows), F32), stack, (1, 1), EXACT)[:1]
    term_got[level] = term_send[...]
    over_column(lambda target: push(term_send, term_got.at[level], 1, target))

    pairs = ctx_size // 2
    wide = [
        jnp.concatenate([got[s, 2 * p], got[s, 2 * p + 1]], axis=1)
        for p in range(pairs)
        for s in range(PLANE_SEQS)
    ]
    wide = jnp.concatenate(wide, axis=0)
    mix = jnp.concatenate([wide[:, :rows], wide[:, 2 * rows : 3 * rows]], axis=1)
    grad = jnp.concatenate([wide[:, rows : 2 * rows], wide[:, 3 * rows :]], axis=1)
    step = PLANE_SEQS * GROUP_SIZE
    state = jnp.zeros((pairs * step, 2 * rows), F32)
    prior = jnp.zeros((pairs * step, 2 * rows), F32)
    for q in range(pairs):
        block = jnp.concatenate(
            [
                taps[:, (2 * q + 1) * rows : (2 * q + 3) * rows],
                taps[:, 2 * q * rows : (2 * q + 2) * rows],
            ],
            axis=0,
        )
        cut = q * step
        ahead = matmul(mix[: pairs * step - cut], block)
        behind = matmul(grad[cut:], block, (1, 1))
        if q == 0:
            state, prior = ahead, behind
        else:
            gap = jnp.zeros((cut, 2 * rows), F32)
            state = state + jnp.concatenate([gap, ahead], axis=0)
            prior = prior + jnp.concatenate([behind, gap], axis=0)
    state = state.astype(BF16)
    prior = prior.astype(BF16)
    for s in range(PLANE_SEQS):
        for i in range(ctx_size):
            first_row = (i // 2) * step + s * GROUP_SIZE
            at = slice(first_row, first_row + GROUP_SIZE)
            span = slice((i % 2) * rows, (i % 2 + 1) * rows)
            back_send[s, i, :, :rows] = state[at, span]
            back_send[s, i, :, rows:] = prior[at, span]
    back_got[channels_of(plane_index)] = back_send[plane_seq, ctx_index]
    over_plane(
        lambda p, s, k, target: push(
            back_send.at[s, k], back_got.at[channels_of(plane_index)], 2, target
        )
    )

    arrived(term_got.at[pl.ds(0, depth - 1)], 1)
    total = term_got[0]
    for i in range(1, depth):
        total = total + term_got[i]
    filter_scale = 1.0 / math.sqrt(data_size * seq_len * GROUP_SIZE)
    at = iota((1, rows), 1)
    small_scale = jnp.where(
        at < modes, filter_scale / math.sqrt(seq_len), 1.0 / math.sqrt(data_size * seq_len)
    )
    small = total[:, seq_len:] * small_scale
    for i in range(ctx_size):
        sum_send[i, :, :rows] = total[:, i * rows : (i + 1) * rows] * filter_scale
        sum_send[i, :, rows:] = small
    sum_got[plane_index] = sum_send[ctx_index]
    over_plane(lambda p, s, k, target: push(sum_send.at[k], sum_got.at[plane_index], 3, target))

    arrived_plane(2)
    results = matmul(unsort[...], back_got[...])
    wide_gate = gate_out[...].astype(F32)
    wide_cot = cotangent[...].astype(F32)
    wide_in = gate_in[...].astype(F32)
    wide_signal = signal[...].astype(F32)
    mixed_wide = (wide_in * wide_signal).astype(BF16).astype(F32)
    back_wide = (wide_cot * wide_gate).astype(BF16).astype(F32)
    mixture = results[:, :rows] + bias_wide[...] * mixed_wide
    conv_out[...] = (wide_gate * mixture).astype(BF16)
    grad_gate_out[...] = (wide_cot * mixture).astype(BF16)
    grad_mixed = results[:, rows:] + bias_wide[...] * back_wide
    grad_gate_in[...] = (grad_mixed * wide_signal).astype(BF16)
    grad_signal[...] = (grad_mixed * wide_in).astype(BF16)

    for store in stores[:4]:
        store.start()

    arrived(sum_got.at[pl.ds(0, groups - 1)], 3)
    for g in range(groups):
        final[g : g + 1, :] = sum_got[g]
    grad_filter[...] = final[:, :rows]
    small = final[:, rows:]
    eye = jnp.where(iota((groups, groups), 0) == iota((groups, groups), 1), 1.0, 0.0)
    grad_residue[...] = matmul(small, eye, (0, 0), EXACT)[:modes]
    spread = matmul(small, jnp.where(member, 1.0, 0.0), (0, 0), EXACT)
    hit = iota((rows, channels), 0).astype(F32) == ranks[...] + modes
    grad_bias[...] = jnp.sum(jnp.where(hit, spread, 0.0), axis=0, keepdims=True)

    for store in stores[4:]:
        store.start()
    for store in stores:
        store.wait()
    sent(sorted_in.at[pl.ds(0, channels - GROUP_SIZE)], 0)
    sent(term_got.at[pl.ds(0, depth - 1)], 1)
    sent(back_got.at[pl.ds(0, channels - GROUP_SIZE)], 2)
    sent(sum_got.at[pl.ds(0, groups - 1)], 3)


def store_kernel(count, *refs):
    sources, results, stages = refs[:count], refs[count : 2 * count], refs[2 * count : 3 * count]
    load_sems, store_sems = refs[3 * count :]
    loads = [
        pltpu.make_async_copy(src, stage, load_sems.at[i])
        for i, (src, stage) in enumerate(zip(sources, stages))
    ]
    stores = [
        pltpu.make_async_copy(stage, dst, store_sems.at[i])
        for i, (stage, dst) in enumerate(zip(stages, results))
    ]
    for load in loads:
        load.start()
    for load, store in zip(loads, stores):
        load.wait()
        store.start()
    for store in stores:
        store.wait()


def body(gate_out, gate_in, signal, cotangent, residue, decay, skip_bias, channel_group):
    data_size = lax.axis_size("dp")
    ctx_size = lax.axis_size("ctx")
    _, channels, rows = gate_out.shape
    groups, modes = residue.shape
    depth = data_size // PLANE_SEQS
    seq_len = rows * ctx_size
    hbm = pl.BlockSpec(memory_space=pltpu.HBM)
    wide = jax.ShapeDtypeStruct((channels, rows), BF16)
    flat = lambda a: a.reshape(channels, rows)
    shapes = [
        wide,
        wide,
        wide,
        wide,
        jax.ShapeDtypeStruct((groups, rows), F32),
        jax.ShapeDtypeStruct((modes, groups), F32),
        jax.ShapeDtypeStruct((1, channels), F32),
    ]
    results = pl.pallas_call(
        functools.partial(kernel, data_size, ctx_size),
        out_shape=shapes,
        in_specs=[hbm] * 8,
        out_specs=[hbm] * len(shapes),
        scratch_shapes=[
            pltpu.VMEM((channels, rows), BF16),
            pltpu.VMEM((channels, rows), BF16),
            pltpu.VMEM((channels, rows), BF16),
            pltpu.VMEM((channels, rows), BF16),
            pltpu.VMEM((modes, groups), F32),
            pltpu.VMEM((modes, groups), F32),
            pltpu.VMEM((1, channels), F32),
            pltpu.VMEM((1, channels), jnp.int32),
            pltpu.SemaphoreType.DMA((8,)),
            *[pltpu.VMEM(a.shape, a.dtype) for a in shapes],
            pltpu.SemaphoreType.DMA((len(shapes),)),
            pltpu.VMEM((channels, 2 * rows), BF16),
            pltpu.VMEM((PLANE_SEQS, ctx_size, GROUP_SIZE, 2 * rows), BF16),
            pltpu.VMEM((channels, channels), BF16),
            pltpu.VMEM((channels, rows), F32),
            pltpu.VMEM((1, channels), F32),
            pltpu.VMEM((modes, seq_len), F32),
            pltpu.VMEM((rows, seq_len + rows), BF16),
            pltpu.VMEM((rows, seq_len + rows), F32),
            pltpu.VMEM((1, seq_len + rows), F32),
            pltpu.VMEM((depth, 1, seq_len + rows), F32),
            pltpu.VMEM((PLANE_SEQS, ctx_size, GROUP_SIZE, 2 * rows), BF16),
            pltpu.VMEM((channels, 2 * rows), BF16),
            pltpu.VMEM((ctx_size, 1, 2 * rows), F32),
            pltpu.VMEM((groups, 1, 2 * rows), F32),
            pltpu.VMEM((groups, 2 * rows), F32),
            pltpu.SemaphoreType.DMA((4,)),
            pltpu.SemaphoreType.DMA((4,)),
        ],
        compiler_params=pltpu.CompilerParams(
            collective_id=0, has_side_effects=True, vmem_limit_bytes=62 * 1024 * 1024
        ),
        cost_estimate=pl.CostEstimate(
            flops=2 * 400_000_000, bytes_accessed=2_000_000, transcendentals=100_000
        ),
    )(
        flat(gate_out),
        flat(gate_in),
        flat(signal),
        flat(cotangent),
        residue.T,
        decay.T,
        skip_bias.reshape(1, channels),
        channel_group.reshape(1, channels),
    )
    results = pl.pallas_call(
        functools.partial(store_kernel, len(shapes)),
        out_shape=shapes,
        in_specs=[hbm] * len(shapes),
        out_specs=[hbm] * len(shapes),
        scratch_shapes=[
            *[pltpu.VMEM(a.shape, a.dtype) for a in shapes],
            pltpu.SemaphoreType.DMA((len(shapes),)),
            pltpu.SemaphoreType.DMA((len(shapes),)),
        ],
    )(*results)
    lifted = tuple(a.reshape(1, channels, rows) for a in results[:4])
    return lifted + (results[4], results[5].T, results[6].reshape(channels))


def solution(mesh):
    return jax.shard_map(
        body,
        mesh=mesh,
        in_specs=(
            P("dp", None, "ctx"),
            P("dp", None, "ctx"),
            P("dp", None, "ctx"),
            P("dp", None, "ctx"),
            P(),
            P(),
            P(),
            P(),
        ),
        out_specs=(
            P("dp", None, "ctx"),
            P("dp", None, "ctx"),
            P("dp", None, "ctx"),
            P("dp", None, "ctx"),
            P(None, "ctx"),
            P(),
            P(),
        ),
        check_vma=False,
    )
```

```python
import functools
import math

import jax
import jax.numpy as jnp
from jax import lax
from jax.experimental import pallas as pl
from jax.experimental.pallas import tpu as pltpu
from jax.sharding import PartitionSpec as P

GROUP_SIZE = 16
PLANE_SEQS = 2
MESH = pl.DeviceIdType.MESH
EXACT = lax.Precision.HIGHEST
F32 = jnp.float32
BF16 = jnp.bfloat16


def iota(shape, dim):
    return lax.broadcasted_iota(jnp.int32, shape, dim)


def matmul(left, right, dims=(1, 0), precision=None):
    return lax.dot_general(
        left,
        right,
        (((dims[0],), (dims[1],)), ((), ())),
        precision=precision,
        preferred_element_type=F32,
    )


def kernel(
    data_size,
    ctx_size,
    gate_out_hbm,
    gate_in_hbm,
    signal_hbm,
    cotangent_hbm,
    residue_hbm,
    decay_hbm,
    skip_bias_hbm,
    channel_group_hbm,
    conv_out_hbm,
    grad_gate_out_hbm,
    grad_gate_in_hbm,
    grad_signal_hbm,
    grad_filter_hbm,
    grad_residue_hbm,
    grad_bias_hbm,
    gate_out,
    gate_in,
    signal,
    cotangent,
    residue,
    decay,
    skip_bias,
    channel_group,
    load_sems,
    conv_out,
    grad_gate_out,
    grad_gate_in,
    grad_signal,
    grad_filter,
    grad_residue,
    grad_bias,
    store_sems,
    sorted_in,
    got,
    unsort,
    bias_wide,
    ranks,
    basis,
    taps,
    lags,
    term_send,
    term_got,
    back_send,
    back_got,
    sum_send,
    sum_got,
    final,
    send_sems,
    recv_sems,
    plane_ready,
    levels_ready,
):
    modes, groups = residue.shape
    channels, rows = gate_out.shape
    seq_len = rows * ctx_size
    depth = data_size // PLANE_SEQS
    blocks = ctx_size * GROUP_SIZE
    ctx_index = lax.axis_index("ctx")
    plane_seq = lax.axis_index("dp") // depth
    level = lax.axis_index("dp") % depth
    plane_index = plane_seq * ctx_size + ctx_index

    wide_y = ctx_size // 4
    here = (ctx_index // 4, 2 * (lax.rem(ctx_index, 4) // 2) + plane_seq, lax.rem(ctx_index, 2))

    def offset(i):
        return jnp.where(i == 2, 3, jnp.where(i == 3, 0, 2 - i))

    def over_plane(step):
        def one(i, c):
            y = lax.rem(here[0] + offset(i // 8 + 4 - wide_y), wide_y)
            x = lax.rem(here[1] + offset(lax.rem(i // 2, 4)), 4)
            rank = 4 * y + 2 * (x // 2) + lax.rem(here[2] + 1 + i, 2)
            seq = lax.rem(x, 2)
            step(seq * ctx_size + rank, seq, rank, {"dp": seq * depth + level, "ctx": rank})
            return c

        lax.fori_loop(0, groups - 1, one, 0)

    def over_column(step):
        def one(i, c):
            o = depth // 2 + (i + 1) // 2 * (1 - 2 * lax.rem(i, 2))
            step({"dp": plane_seq * depth + lax.rem(level + o, depth)})
            return c

        lax.fori_loop(0, depth - 1, one, 0)

    def push(src, dst, phase, target):
        pltpu.make_async_remote_copy(
            src_ref=src,
            dst_ref=dst,
            send_sem=send_sems.at[phase],
            recv_sem=recv_sems.at[phase],
            device_id=target,
            device_id_type=MESH,
        ).start()

    def arrived(span, phase):
        pltpu.make_async_copy(span, span, recv_sems.at[phase]).wait()

    def sent(span, phase):
        pltpu.make_async_copy(span, span, send_sems.at[phase]).wait()

    def arrived_plane(phase):
        span = sorted_in.at[pl.ds(0, channels - GROUP_SIZE)]
        arrived(span, phase)

    loads = [
        pltpu.make_async_copy(src, dst, load_sems.at[i])
        for i, (src, dst) in enumerate(
            [
                (channel_group_hbm, channel_group),
                (gate_in_hbm, gate_in),
                (signal_hbm, signal),
                (gate_out_hbm, gate_out),
                (cotangent_hbm, cotangent),
                (decay_hbm, decay),
                (residue_hbm, residue),
                (skip_bias_hbm, skip_bias),
            ]
        )
    ]
    for load in loads:
        load.start()
    stores = [
        pltpu.make_async_copy(src, dst, store_sems.at[i])
        for i, (src, dst) in enumerate(
            [
                (conv_out, conv_out_hbm),
                (grad_gate_out, grad_gate_out_hbm),
                (grad_gate_in, grad_gate_in_hbm),
                (grad_signal, grad_signal_hbm),
                (grad_filter, grad_filter_hbm),
                (grad_residue, grad_residue_hbm),
                (grad_bias, grad_bias_hbm),
            ]
        )
    ]

    barrier = pltpu.get_barrier_semaphore()
    core = lax.rem(ctx_index, 2)
    mate = {"ctx": ctx_index + 1 - 2 * core}

    def greet_plane(p, s, k, target):
        @pl.when(lax.rem(k, 2) == 0)
        def _():
            pl.semaphore_signal(barrier, inc=1, device_id=target, device_id_type=MESH)

    over_plane(greet_plane)
    over_column(
        lambda target: pl.semaphore_signal(
            barrier,
            inc=1,
            device_id={"dp": target["dp"], "ctx": ctx_index + 1 - core},
            device_id_type=MESH,
        )
    )

    loads[0].wait()
    member = iota((groups, channels), 0) == channel_group[...]
    before = jnp.where(iota((channels, channels), 0) < iota((channels, channels), 1), 1.0, 0.0)
    rank = matmul(jnp.where(member, 1.0, 0.0).astype(BF16), before.astype(BF16))
    rank = jnp.sum(jnp.where(member, rank, 0.0), axis=0, keepdims=True)
    ranks[...] = rank
    first = jnp.sum(
        jnp.where(member, iota((groups, channels), 0).astype(F32), 0.0), axis=0, keepdims=True
    )
    place = first * GROUP_SIZE + rank
    sort = jnp.where(iota((channels, channels), 0).astype(F32) == place, 1.0, 0.0).astype(BF16)

    for load in loads[1:5]:
        load.wait()
    mixed = (gate_in[...].astype(F32) * signal[...].astype(F32)).astype(BF16)
    back = (cotangent[...].astype(F32) * gate_out[...].astype(F32)).astype(BF16)
    sorted_in[...] = matmul(sort, jnp.concatenate([mixed, back], axis=1)).astype(BF16)

    def channels_of(peer):
        return pl.ds(pl.multiple_of(peer * GROUP_SIZE, GROUP_SIZE), GROUP_SIZE)

    got[plane_seq, ctx_index] = sorted_in[channels_of(plane_index)]

    @pl.when(core == 0)
    def _():
        pl.semaphore_wait(barrier, groups - 1)
        pl.semaphore_signal(plane_ready, inc=1, device_id=mate, device_id_type=MESH)

    @pl.when(core == 1)
    def _():
        pl.semaphore_wait(plane_ready, 1)

    over_plane(
        lambda p, s, k, target: push(
            sorted_in.at[channels_of(p)], got.at[plane_seq, ctx_index], 0, target
        )
    )

    for load in loads[5:]:
        load.wait()
    place_wide = jnp.transpose(jnp.broadcast_to(place, (128, channels)))
    unsort[...] = jnp.where(
        iota((channels, channels), 1).astype(F32) == place_wide[:, :1], 1.0, 0.0
    ).astype(BF16)
    bias_wide[...] = jnp.transpose(jnp.broadcast_to(skip_bias[...], (rows, channels)))
    lane = iota((modes, rows), 1).astype(F32)
    pick = jnp.where(iota((groups, rows), 0) == plane_index, 1.0, 0.0)
    rate = matmul(decay[...], pick, precision=EXACT)
    weight = matmul(residue[...], pick, precision=EXACT)
    for i in range(ctx_size):
        basis[:, i * rows : (i + 1) * rows] = jnp.exp(-rate * ((lane + i * rows) / seq_len))
    filt = matmul(weight * jnp.exp(rate * (lane / seq_len)), basis[...], (0, 0), EXACT)
    causal = iota((rows, rows), 1) >= iota((rows, rows), 0)
    taps[:, :rows] = jnp.zeros((rows, rows), BF16)
    taps[:, rows : 2 * rows] = jnp.where(causal, filt[:, :rows], 0.0).astype(BF16)
    taps[:, 2 * rows :] = filt[:, rows:].astype(BF16)

    @pl.when(core == 1)
    def _():
        pl.semaphore_wait(barrier, 2 * (depth - 1))
        pl.semaphore_signal(levels_ready, inc=1, device_id=mate, device_id_type=MESH)

    arrived_plane(0)

    mixes = [got[s, :, :, :rows].reshape(blocks, rows) for s in range(PLANE_SEQS)]
    grads = [got[s, :, :, rows:].reshape(blocks, rows) for s in range(PLANE_SEQS)]
    mix_t = jnp.transpose(jnp.concatenate(mixes, axis=0))

    def shifted(k):
        if k == 0:
            return jnp.concatenate(grads, axis=0)
        gap = jnp.zeros((k * GROUP_SIZE, rows), BF16)
        return jnp.concatenate([x for a in grads for x in (a[k * GROUP_SIZE :], gap)], axis=0)

    for k in range(0, ctx_size, 2):
        pair = jnp.concatenate([shifted(k), shifted(k + 1)], axis=1)
        lags[:, k * rows : (k + 2) * rows] = matmul(mix_t, pair)
    width = seq_len + rows
    lags[:, seq_len:] = jnp.zeros((rows, rows), F32)
    parts = [lags[a * 8 : (a + 1) * 8, :] for a in range(rows // 8)]
    shift = 8
    while len(parts) > 1:
        parts = [
            parts[a] + pltpu.roll(parts[a + 1], width - shift, 1) for a in range(0, len(parts), 2)
        ]
        shift *= 2
    skew = parts[0]
    row = iota((8, width), 0)
    for bit in (1, 2, 4):
        skew = jnp.where(row & bit != 0, pltpu.roll(skew, width - bit, 1), skew)
    corr = jnp.sum(skew, axis=0, keepdims=True)
    modal = jnp.zeros((modes, rows), F32)
    direct = jnp.zeros((GROUP_SIZE, rows), F32)
    for i in range(ctx_size):
        span = slice(i * rows, (i + 1) * rows)
        modal = modal + basis[:, span] * corr[:, span]
        for s in range(PLANE_SEQS):
            direct = direct + got[s, i, :, :rows].astype(F32) * got[s, i, :, rows:].astype(F32)
    stack = jnp.concatenate(
        [modal, direct, jnp.zeros((rows - modes - GROUP_SIZE, rows), F32)], axis=0
    )
    term_send[:, :seq_len] = corr[:, :seq_len]
    term_send[:, seq_len:] = matmul(jnp.ones((8, rows), F32), stack, (1, 1), EXACT)[:1]
    term_got[level] = term_send[...]

    @pl.when(core == 0)
    def _():
        pl.semaphore_wait(levels_ready, 1)

    over_column(lambda target: push(term_send, term_got.at[level], 1, target))

    pairs = ctx_size // 2
    wide = [
        jnp.concatenate([got[s, 2 * p], got[s, 2 * p + 1]], axis=1)
        for p in range(pairs)
        for s in range(PLANE_SEQS)
    ]
    wide = jnp.concatenate(wide, axis=0)
    mix = jnp.concatenate([wide[:, :rows], wide[:, 2 * rows : 3 * rows]], axis=1)
    grad = jnp.concatenate([wide[:, rows : 2 * rows], wide[:, 3 * rows :]], axis=1)
    step = PLANE_SEQS * GROUP_SIZE
    state = jnp.zeros((pairs * step, 2 * rows), F32)
    prior = jnp.zeros((pairs * step, 2 * rows), F32)
    for q in range(pairs):
        block = jnp.concatenate(
            [
                taps[:, (2 * q + 1) * rows : (2 * q + 3) * rows],
                taps[:, 2 * q * rows : (2 * q + 2) * rows],
            ],
            axis=0,
        )
        cut = q * step
        ahead = matmul(mix[: pairs * step - cut], block)
        behind = matmul(grad[cut:], block, (1, 1))
        if q == 0:
            state, prior = ahead, behind
        else:
            gap = jnp.zeros((cut, 2 * rows), F32)
            state = state + jnp.concatenate([gap, ahead], axis=0)
            prior = prior + jnp.concatenate([behind, gap], axis=0)
    state = state.astype(BF16)
    prior = prior.astype(BF16)
    for s in range(PLANE_SEQS):
        for i in range(ctx_size):
            first_row = (i // 2) * step + s * GROUP_SIZE
            at = slice(first_row, first_row + GROUP_SIZE)
            span = slice((i % 2) * rows, (i % 2 + 1) * rows)
            back_send[s, i, :, :rows] = state[at, span]
            back_send[s, i, :, rows:] = prior[at, span]
    back_got[channels_of(plane_index)] = back_send[plane_seq, ctx_index]
    over_plane(
        lambda p, s, k, target: push(
            back_send.at[s, k], back_got.at[channels_of(plane_index)], 2, target
        )
    )

    arrived(term_got.at[pl.ds(0, depth - 1)], 1)
    total = term_got[0]
    for i in range(1, depth):
        total = total + term_got[i]
    filter_scale = 1.0 / math.sqrt(data_size * seq_len * GROUP_SIZE)
    at = iota((1, rows), 1)
    small_scale = jnp.where(
        at < modes, filter_scale / math.sqrt(seq_len), 1.0 / math.sqrt(data_size * seq_len)
    )
    small = total[:, seq_len:] * small_scale
    for i in range(ctx_size):
        sum_send[i, :, :rows] = total[:, i * rows : (i + 1) * rows] * filter_scale
        sum_send[i, :, rows:] = small
    sum_got[plane_index] = sum_send[ctx_index]
    over_plane(lambda p, s, k, target: push(sum_send.at[k], sum_got.at[plane_index], 3, target))

    arrived_plane(2)
    results = matmul(unsort[...], back_got[...])
    wide_gate = gate_out[...].astype(F32)
    wide_cot = cotangent[...].astype(F32)
    wide_in = gate_in[...].astype(F32)
    wide_signal = signal[...].astype(F32)
    mixed_wide = (wide_in * wide_signal).astype(BF16).astype(F32)
    back_wide = (wide_cot * wide_gate).astype(BF16).astype(F32)
    mixture = results[:, :rows] + bias_wide[...] * mixed_wide
    conv_out[...] = (wide_gate * mixture).astype(BF16)
    grad_gate_out[...] = (wide_cot * mixture).astype(BF16)
    grad_mixed = results[:, rows:] + bias_wide[...] * back_wide
    grad_gate_in[...] = (grad_mixed * wide_signal).astype(BF16)
    grad_signal[...] = (grad_mixed * wide_in).astype(BF16)

    for store in stores[:4]:
        store.start()

    arrived(sum_got.at[pl.ds(0, groups - 1)], 3)
    for g in range(groups):
        final[g : g + 1, :] = sum_got[g]
    grad_filter[...] = final[:, :rows]
    small = final[:, rows:]
    eye = jnp.where(iota((groups, groups), 0) == iota((groups, groups), 1), 1.0, 0.0)
    grad_residue[...] = matmul(small, eye, (0, 0), EXACT)[:modes]
    spread = matmul(small, jnp.where(member, 1.0, 0.0), (0, 0), EXACT)
    hit = iota((rows, channels), 0).astype(F32) == ranks[...] + modes
    grad_bias[...] = jnp.sum(jnp.where(hit, spread, 0.0), axis=0, keepdims=True)

    for store in stores[4:]:
        store.start()
    for store in stores:
        store.wait()
    sent(sorted_in.at[pl.ds(0, channels - GROUP_SIZE)], 0)
    sent(term_got.at[pl.ds(0, depth - 1)], 1)
    sent(back_got.at[pl.ds(0, channels - GROUP_SIZE)], 2)
    sent(sum_got.at[pl.ds(0, groups - 1)], 3)


def store_kernel(count, *refs):
    sources, results, stages = refs[:count], refs[count : 2 * count], refs[2 * count : 3 * count]
    load_sems, store_sems = refs[3 * count :]
    loads = [
        pltpu.make_async_copy(src, stage, load_sems.at[i])
        for i, (src, stage) in enumerate(zip(sources, stages))
    ]
    stores = [
        pltpu.make_async_copy(stage, dst, store_sems.at[i])
        for i, (stage, dst) in enumerate(zip(stages, results))
    ]
    for load in loads:
        load.start()
    for load, store in zip(loads, stores):
        load.wait()
        store.start()
    for store in stores:
        store.wait()


def body(gate_out, gate_in, signal, cotangent, residue, decay, skip_bias, channel_group):
    data_size = lax.axis_size("dp")
    ctx_size = lax.axis_size("ctx")
    _, channels, rows = gate_out.shape
    groups, modes = residue.shape
    depth = data_size // PLANE_SEQS
    seq_len = rows * ctx_size
    hbm = pl.BlockSpec(memory_space=pltpu.HBM)
    wide = jax.ShapeDtypeStruct((channels, rows), BF16)
    flat = lambda a: a.reshape(channels, rows)
    shapes = [
        wide,
        wide,
        wide,
        wide,
        jax.ShapeDtypeStruct((groups, rows), F32),
        jax.ShapeDtypeStruct((modes, groups), F32),
        jax.ShapeDtypeStruct((1, channels), F32),
    ]
    results = pl.pallas_call(
        functools.partial(kernel, data_size, ctx_size),
        out_shape=shapes,
        in_specs=[hbm] * 8,
        out_specs=[hbm] * len(shapes),
        scratch_shapes=[
            pltpu.VMEM((channels, rows), BF16),
            pltpu.VMEM((channels, rows), BF16),
            pltpu.VMEM((channels, rows), BF16),
            pltpu.VMEM((channels, rows), BF16),
            pltpu.VMEM((modes, groups), F32),
            pltpu.VMEM((modes, groups), F32),
            pltpu.VMEM((1, channels), F32),
            pltpu.VMEM((1, channels), jnp.int32),
            pltpu.SemaphoreType.DMA((8,)),
            *[pltpu.VMEM(a.shape, a.dtype) for a in shapes],
            pltpu.SemaphoreType.DMA((len(shapes),)),
            pltpu.VMEM((channels, 2 * rows), BF16),
            pltpu.VMEM((PLANE_SEQS, ctx_size, GROUP_SIZE, 2 * rows), BF16),
            pltpu.VMEM((channels, channels), BF16),
            pltpu.VMEM((channels, rows), F32),
            pltpu.VMEM((1, channels), F32),
            pltpu.VMEM((modes, seq_len), F32),
            pltpu.VMEM((rows, seq_len + rows), BF16),
            pltpu.VMEM((rows, seq_len + rows), F32),
            pltpu.VMEM((1, seq_len + rows), F32),
            pltpu.VMEM((depth, 1, seq_len + rows), F32),
            pltpu.VMEM((PLANE_SEQS, ctx_size, GROUP_SIZE, 2 * rows), BF16),
            pltpu.VMEM((channels, 2 * rows), BF16),
            pltpu.VMEM((ctx_size, 1, 2 * rows), F32),
            pltpu.VMEM((groups, 1, 2 * rows), F32),
            pltpu.VMEM((groups, 2 * rows), F32),
            pltpu.SemaphoreType.DMA((4,)),
            pltpu.SemaphoreType.DMA((4,)),
            pltpu.SemaphoreType.REGULAR,
            pltpu.SemaphoreType.REGULAR,
        ],
        compiler_params=pltpu.CompilerParams(
            collective_id=0, has_side_effects=True, vmem_limit_bytes=62 * 1024 * 1024
        ),
        cost_estimate=pl.CostEstimate(
            flops=2 * 400_000_000, bytes_accessed=2_000_000, transcendentals=100_000
        ),
    )(
        flat(gate_out),
        flat(gate_in),
        flat(signal),
        flat(cotangent),
        residue.T,
        decay.T,
        skip_bias.reshape(1, channels),
        channel_group.reshape(1, channels),
    )
    results = pl.pallas_call(
        functools.partial(store_kernel, len(shapes)),
        out_shape=shapes,
        in_specs=[hbm] * len(shapes),
        out_specs=[hbm] * len(shapes),
        scratch_shapes=[
            *[pltpu.VMEM(a.shape, a.dtype) for a in shapes],
            pltpu.SemaphoreType.DMA((len(shapes),)),
            pltpu.SemaphoreType.DMA((len(shapes),)),
        ],
    )(*results)
    lifted = tuple(a.reshape(1, channels, rows) for a in results[:4])
    return lifted + (results[4], results[5].T, results[6].reshape(channels))


def solution(mesh):
    return jax.shard_map(
        body,
        mesh=mesh,
        in_specs=(
            P("dp", None, "ctx"),
            P("dp", None, "ctx"),
            P("dp", None, "ctx"),
            P("dp", None, "ctx"),
            P(),
            P(),
            P(),
            P(),
        ),
        out_specs=(
            P("dp", None, "ctx"),
            P("dp", None, "ctx"),
            P("dp", None, "ctx"),
            P("dp", None, "ctx"),
            P(None, "ctx"),
            P(),
            P(),
        ),
        check_vma=False,
    )
```

```python
import functools
import math

import jax
import jax.numpy as jnp
from jax import lax
from jax.experimental import pallas as pl
from jax.experimental.pallas import tpu as pltpu
from jax.sharding import PartitionSpec as P

GROUP_SIZE = 16
PLANE_SEQS = 2
MESH = pl.DeviceIdType.MESH
EXACT = lax.Precision.HIGHEST
F32 = jnp.float32
BF16 = jnp.bfloat16


def iota(shape, dim):
    return lax.broadcasted_iota(jnp.int32, shape, dim)


def matmul(left, right, dims=(1, 0), precision=None):
    return lax.dot_general(
        left,
        right,
        (((dims[0],), (dims[1],)), ((), ())),
        precision=precision,
        preferred_element_type=F32,
    )


def kernel(
    data_size,
    ctx_size,
    gate_out_hbm,
    gate_in_hbm,
    signal_hbm,
    cotangent_hbm,
    residue_hbm,
    decay_hbm,
    skip_bias_hbm,
    channel_group_hbm,
    conv_out,
    grad_gate_out,
    grad_gate_in,
    grad_signal,
    grad_filter,
    grad_residue,
    grad_bias,
    gate_out,
    gate_in,
    signal,
    cotangent,
    residue,
    decay,
    skip_bias,
    channel_group,
    load_sems,
    sorted_in,
    got,
    unsort,
    bias_wide,
    ranks,
    basis,
    taps,
    lags,
    lag_rows,
    term_send,
    term_got,
    small_send,
    small_got,
    back_send,
    back_got,
    sum_send,
    sum_got,
    final,
    send_sems,
    recv_sems,
    plane_ready,
    levels_ready,
):
    modes, groups = residue.shape
    channels, rows = gate_out.shape
    seq_len = rows * ctx_size
    depth = data_size // PLANE_SEQS
    blocks = ctx_size * GROUP_SIZE
    ctx_index = lax.axis_index("ctx")
    plane_seq = lax.axis_index("dp") // depth
    level = lax.axis_index("dp") % depth
    plane_index = plane_seq * ctx_size + ctx_index

    wide_y = ctx_size // 4
    here = (ctx_index // 4, 2 * (lax.rem(ctx_index, 4) // 2) + plane_seq, lax.rem(ctx_index, 2))

    def offset(i):
        return jnp.where(i == 2, 3, jnp.where(i == 3, 0, 2 - i))

    def over_plane(step):
        def one(i, c):
            y = lax.rem(here[0] + offset(i // 8 + 4 - wide_y), wide_y)
            x = lax.rem(here[1] + offset(lax.rem(i // 2, 4)), 4)
            rank = 4 * y + 2 * (x // 2) + lax.rem(here[2] + 1 + i, 2)
            seq = lax.rem(x, 2)
            step(seq * ctx_size + rank, seq, rank, {"dp": seq * depth + level, "ctx": rank})
            return c

        lax.fori_loop(0, groups - 1, one, 0)

    def over_column(step):
        def one(i, c):
            o = depth // 2 + (i + 1) // 2 * (1 - 2 * lax.rem(i, 2))
            step({"dp": plane_seq * depth + lax.rem(level + o, depth)})
            return c

        lax.fori_loop(0, depth - 1, one, 0)

    def push(src, dst, phase, target):
        pltpu.make_async_remote_copy(
            src_ref=src,
            dst_ref=dst,
            send_sem=send_sems.at[phase],
            recv_sem=recv_sems.at[phase],
            device_id=target,
            device_id_type=MESH,
        ).start()

    def arrived(span, phase):
        pltpu.make_async_copy(span, span, recv_sems.at[phase]).wait()

    def sent(span, phase):
        pltpu.make_async_copy(span, span, send_sems.at[phase]).wait()

    def arrived_plane(phase):
        span = sorted_in.at[pl.ds(0, channels - GROUP_SIZE)]
        arrived(span, phase)

    loads = [
        pltpu.make_async_copy(src, dst, load_sems.at[i])
        for i, (src, dst) in enumerate(
            [
                (channel_group_hbm, channel_group),
                (gate_in_hbm, gate_in),
                (signal_hbm, signal),
                (gate_out_hbm, gate_out),
                (cotangent_hbm, cotangent),
                (decay_hbm, decay),
                (residue_hbm, residue),
                (skip_bias_hbm, skip_bias),
            ]
        )
    ]
    for load in loads:
        load.start()

    barrier = pltpu.get_barrier_semaphore()
    core = lax.rem(ctx_index, 2)
    mate = {"ctx": ctx_index + 1 - 2 * core}

    def greet_plane(p, s, k, target):
        @pl.when(lax.rem(k, 2) == 0)
        def _():
            pl.semaphore_signal(barrier, inc=1, device_id=target, device_id_type=MESH)

    over_plane(greet_plane)
    over_column(
        lambda target: pl.semaphore_signal(
            barrier,
            inc=1,
            device_id={"dp": target["dp"], "ctx": ctx_index + 1 - core},
            device_id_type=MESH,
        )
    )

    loads[0].wait()
    member = iota((groups, channels), 0) == channel_group[...]
    before = jnp.where(iota((channels, channels), 0) < iota((channels, channels), 1), 1.0, 0.0)
    rank = matmul(jnp.where(member, 1.0, 0.0).astype(BF16), before.astype(BF16))
    rank = jnp.sum(jnp.where(member, rank, 0.0), axis=0, keepdims=True)
    ranks[...] = rank
    first = jnp.sum(
        jnp.where(member, iota((groups, channels), 0).astype(F32), 0.0), axis=0, keepdims=True
    )
    place = first * GROUP_SIZE + rank
    sort = jnp.where(iota((channels, channels), 0).astype(F32) == place, 1.0, 0.0).astype(BF16)

    for load in loads[1:5]:
        load.wait()
    mixed = (gate_in[...].astype(F32) * signal[...].astype(F32)).astype(BF16)
    back = (cotangent[...].astype(F32) * gate_out[...].astype(F32)).astype(BF16)
    sorted_in[...] = matmul(sort, jnp.concatenate([mixed, back], axis=1)).astype(BF16)

    def channels_of(peer):
        return pl.ds(pl.multiple_of(peer * GROUP_SIZE, GROUP_SIZE), GROUP_SIZE)

    got[plane_seq, ctx_index] = sorted_in[channels_of(plane_index)]

    @pl.when(core == 0)
    def _():
        pl.semaphore_wait(barrier, groups - 1)
        pl.semaphore_signal(plane_ready, inc=1, device_id=mate, device_id_type=MESH)

    @pl.when(core == 1)
    def _():
        pl.semaphore_wait(plane_ready, 1)

    over_plane(
        lambda p, s, k, target: push(
            sorted_in.at[channels_of(p)], got.at[plane_seq, ctx_index], 0, target
        )
    )

    for load in loads[5:]:
        load.wait()
    place_wide = jnp.transpose(jnp.broadcast_to(place, (128, channels)))
    unsort[...] = jnp.where(
        iota((channels, channels), 1).astype(F32) == place_wide[:, :1], 1.0, 0.0
    ).astype(BF16)
    bias_wide[...] = jnp.transpose(jnp.broadcast_to(skip_bias[...], (rows, channels)))
    lane = iota((modes, rows), 1).astype(F32)
    pick = jnp.where(iota((groups, rows), 0) == plane_index, 1.0, 0.0)
    rate = matmul(decay[...], pick, precision=EXACT)
    weight = matmul(residue[...], pick, precision=EXACT)
    for i in range(ctx_size):
        basis[:, i * rows : (i + 1) * rows] = jnp.exp(-rate * ((lane + i * rows) / seq_len))
    filt = matmul(weight * jnp.exp(rate * (lane / seq_len)), basis[...], (0, 0), EXACT)
    causal = iota((rows, rows), 1) >= iota((rows, rows), 0)
    taps[:, :rows] = jnp.zeros((rows, rows), BF16)
    taps[:, rows : 2 * rows] = jnp.where(causal, filt[:, :rows], 0.0).astype(BF16)
    taps[:, 2 * rows :] = filt[:, rows:].astype(BF16)

    @pl.when(core == 1)
    def _():
        pl.semaphore_wait(barrier, 2 * (depth - 1))
        pl.semaphore_signal(levels_ready, inc=1, device_id=mate, device_id_type=MESH)

    arrived_plane(0)

    mixes = [got[s, :, :, :rows].reshape(blocks, rows) for s in range(PLANE_SEQS)]
    grads = [got[s, :, :, rows:].reshape(blocks, rows) for s in range(PLANE_SEQS)]
    mix_t = jnp.transpose(jnp.concatenate(mixes, axis=0))

    def shifted(k):
        if k == 0:
            return jnp.concatenate(grads, axis=0)
        gap = jnp.zeros((k * GROUP_SIZE, rows), BF16)
        return jnp.concatenate([x for a in grads for x in (a[k * GROUP_SIZE :], gap)], axis=0)

    for k in range(0, ctx_size, 2):
        pair = jnp.concatenate([shifted(k), shifted(k + 1)], axis=1)
        lags[:, k * rows : (k + 2) * rows] = matmul(mix_t, pair)
    width = seq_len + rows
    lags[:, seq_len:] = jnp.zeros((rows, rows), F32)
    parts = [lags[a * 8 : (a + 1) * 8, :] for a in range(rows // 8)]
    shift = 8
    while len(parts) > 1:
        parts = [
            parts[a] + pltpu.roll(parts[a + 1], width - shift, 1) for a in range(0, len(parts), 2)
        ]
        shift *= 2
    skew = parts[0]
    row = iota((8, width), 0)
    for bit in (1, 2, 4):
        skew = jnp.where(row & bit != 0, pltpu.roll(skew, width - bit, 1), skew)
    corr = jnp.sum(skew, axis=0, keepdims=True)
    modal = jnp.zeros((modes, rows), F32)
    direct = jnp.zeros((GROUP_SIZE, rows), F32)
    for i in range(ctx_size):
        span = slice(i * rows, (i + 1) * rows)
        modal = modal + basis[:, span] * corr[:, span]
        lag_rows[i : i + 1, :] = corr[:, span]
        for s in range(PLANE_SEQS):
            direct = direct + got[s, i, :, :rows].astype(F32) * got[s, i, :, rows:].astype(F32)
    stack = jnp.concatenate(
        [modal, direct, jnp.zeros((rows - modes - GROUP_SIZE, rows), F32)], axis=0
    )
    term_send[...] = lag_rows[...].astype(BF16)
    small_send[...] = matmul(jnp.ones((8, rows), F32), stack, (1, 1), EXACT)[:1]
    term_got[level] = term_send[...]
    small_got[level] = small_send[...]

    @pl.when(core == 0)
    def _():
        pl.semaphore_wait(levels_ready, 1)


    def push_terms(target):
        push(term_send, term_got.at[level], 1, target)
        push(small_send, small_got.at[level], 4, target)

    over_column(push_terms)

    pairs = ctx_size // 2
    wide = [
        jnp.concatenate([got[s, 2 * p], got[s, 2 * p + 1]], axis=1)
        for p in range(pairs)
        for s in range(PLANE_SEQS)
    ]
    wide = jnp.concatenate(wide, axis=0)
    mix = jnp.concatenate([wide[:, :rows], wide[:, 2 * rows : 3 * rows]], axis=1)
    grad = jnp.concatenate([wide[:, rows : 2 * rows], wide[:, 3 * rows :]], axis=1)
    step = PLANE_SEQS * GROUP_SIZE
    state = jnp.zeros((pairs * step, 2 * rows), F32)
    prior = jnp.zeros((pairs * step, 2 * rows), F32)
    for q in range(pairs):
        block = jnp.concatenate(
            [
                taps[:, (2 * q + 1) * rows : (2 * q + 3) * rows],
                taps[:, 2 * q * rows : (2 * q + 2) * rows],
            ],
            axis=0,
        )
        cut = q * step
        ahead = matmul(mix[: pairs * step - cut], block)
        behind = matmul(grad[cut:], block, (1, 1))
        if q == 0:
            state, prior = ahead, behind
        else:
            gap = jnp.zeros((cut, 2 * rows), F32)
            state = state + jnp.concatenate([gap, ahead], axis=0)
            prior = prior + jnp.concatenate([behind, gap], axis=0)
    state = state.astype(BF16)
    prior = prior.astype(BF16)
    for s in range(PLANE_SEQS):
        for i in range(ctx_size):
            first_row = (i // 2) * step + s * GROUP_SIZE
            at = slice(first_row, first_row + GROUP_SIZE)
            span = slice((i % 2) * rows, (i % 2 + 1) * rows)
            back_send[s, i, :, :rows] = state[at, span]
            back_send[s, i, :, rows:] = prior[at, span]
    back_got[channels_of(plane_index)] = back_send[plane_seq, ctx_index]
    over_plane(
        lambda p, s, k, target: push(
            back_send.at[s, k], back_got.at[channels_of(plane_index)], 2, target
        )
    )

    arrived(term_got.at[pl.ds(0, depth - 1)], 1)
    total = term_got[0].astype(F32)
    for i in range(1, depth):
        total = total + term_got[i].astype(F32)
    arrived(small_got.at[pl.ds(0, depth - 1)], 4)
    small = small_got[0]
    for i in range(1, depth):
        small = small + small_got[i]
    filter_scale = 1.0 / math.sqrt(data_size * seq_len * GROUP_SIZE)
    at = iota((1, rows), 1)
    small_scale = jnp.where(
        at < modes, filter_scale / math.sqrt(seq_len), 1.0 / math.sqrt(data_size * seq_len)
    )
    small = small * small_scale
    total = total * filter_scale
    for i in range(ctx_size):
        sum_send[i, :, :rows] = total[i : i + 1]
        sum_send[i, :, rows:] = small
    sum_got[plane_index] = sum_send[ctx_index]
    over_plane(lambda p, s, k, target: push(sum_send.at[k], sum_got.at[plane_index], 3, target))

    arrived_plane(2)
    results = matmul(unsort[...], back_got[...])
    wide_gate = gate_out[...].astype(F32)
    wide_cot = cotangent[...].astype(F32)
    wide_in = gate_in[...].astype(F32)
    wide_signal = signal[...].astype(F32)
    mixed_wide = (wide_in * wide_signal).astype(BF16).astype(F32)
    back_wide = (wide_cot * wide_gate).astype(BF16).astype(F32)
    mixture = results[:, :rows] + bias_wide[...] * mixed_wide
    conv_out[...] = (wide_gate * mixture).astype(BF16)
    grad_gate_out[...] = (wide_cot * mixture).astype(BF16)
    grad_mixed = results[:, rows:] + bias_wide[...] * back_wide
    grad_gate_in[...] = (grad_mixed * wide_signal).astype(BF16)
    grad_signal[...] = (grad_mixed * wide_in).astype(BF16)

    arrived(sum_got.at[pl.ds(0, groups - 1)], 3)
    for g in range(groups):
        final[g : g + 1, :] = sum_got[g]
    grad_filter[...] = final[:, :rows]
    small = jnp.transpose(final[:, rows:])
    grad_residue[...] = small[:modes]
    terms = small[modes : modes + GROUP_SIZE]
    upper = terms.astype(BF16)
    middle = (terms - upper.astype(F32)).astype(BF16)
    lower = (terms - upper.astype(F32) - middle.astype(F32)).astype(BF16)
    spread = matmul(
        jnp.concatenate([upper, middle, lower], axis=0), jnp.where(member, 1.0, 0.0).astype(BF16)
    )
    spread = (
        spread[:GROUP_SIZE] + spread[GROUP_SIZE : 2 * GROUP_SIZE] + spread[2 * GROUP_SIZE :]
    )
    hit = iota((GROUP_SIZE, channels), 0).astype(F32) == ranks[...]
    grad_bias[...] = jnp.sum(jnp.where(hit, spread, 0.0), axis=0, keepdims=True)

    sent(sorted_in.at[pl.ds(0, channels - GROUP_SIZE)], 0)
    sent(term_got.at[pl.ds(0, depth - 1)], 1)
    sent(small_got.at[pl.ds(0, depth - 1)], 4)
    sent(back_got.at[pl.ds(0, channels - GROUP_SIZE)], 2)
    sent(sum_got.at[pl.ds(0, groups - 1)], 3)


def store_kernel(count, *refs):
    sources, results, sems = refs[:count], refs[count : 2 * count], refs[2 * count]
    stores = [
        pltpu.make_async_copy(src, dst, sems.at[i])
        for i, (src, dst) in enumerate(zip(sources, results))
    ]
    for store in stores:
        store.start()
    for store in stores:
        store.wait()


def body(gate_out, gate_in, signal, cotangent, residue, decay, skip_bias, channel_group):
    data_size = lax.axis_size("dp")
    ctx_size = lax.axis_size("ctx")
    _, channels, rows = gate_out.shape
    groups, modes = residue.shape
    depth = data_size // PLANE_SEQS
    seq_len = rows * ctx_size
    vmem = pl.BlockSpec(memory_space=pltpu.VMEM)
    hbm = pl.BlockSpec(memory_space=pltpu.HBM)
    wide = jax.ShapeDtypeStruct((channels, rows), BF16)
    flat = lambda a: a.reshape(channels, rows)
    shapes = [
        wide,
        wide,
        wide,
        wide,
        jax.ShapeDtypeStruct((groups, rows), F32),
        jax.ShapeDtypeStruct((modes, groups), F32),
        jax.ShapeDtypeStruct((1, channels), F32),
    ]
    results = pl.pallas_call(
        functools.partial(kernel, data_size, ctx_size),
        out_shape=[pltpu.VMEM(a.shape, a.dtype) for a in shapes],
        in_specs=[hbm] * 8,
        out_specs=[vmem] * len(shapes),
        scratch_shapes=[
            pltpu.VMEM((channels, rows), BF16),
            pltpu.VMEM((channels, rows), BF16),
            pltpu.VMEM((channels, rows), BF16),
            pltpu.VMEM((channels, rows), BF16),
            pltpu.VMEM((modes, groups), F32),
            pltpu.VMEM((modes, groups), F32),
            pltpu.VMEM((1, channels), F32),
            pltpu.VMEM((1, channels), jnp.int32),
            pltpu.SemaphoreType.DMA((8,)),
            pltpu.VMEM((channels, 2 * rows), BF16),
            pltpu.VMEM((PLANE_SEQS, ctx_size, GROUP_SIZE, 2 * rows), BF16),
            pltpu.VMEM((channels, channels), BF16),
            pltpu.VMEM((channels, rows), F32),
            pltpu.VMEM((1, channels), F32),
            pltpu.VMEM((modes, seq_len), F32),
            pltpu.VMEM((rows, seq_len + rows), BF16),
            pltpu.VMEM((rows, seq_len + rows), F32),
            pltpu.VMEM((ctx_size, rows), F32),
            pltpu.VMEM((ctx_size, rows), BF16),
            pltpu.VMEM((depth, ctx_size, rows), BF16),
            pltpu.VMEM((1, rows), F32),
            pltpu.VMEM((depth, 1, rows), F32),
            pltpu.VMEM((PLANE_SEQS, ctx_size, GROUP_SIZE, 2 * rows), BF16),
            pltpu.VMEM((channels, 2 * rows), BF16),
            pltpu.VMEM((ctx_size, 1, 2 * rows), F32),
            pltpu.VMEM((groups, 1, 2 * rows), F32),
            pltpu.VMEM((groups, 2 * rows), F32),
            pltpu.SemaphoreType.DMA((5,)),
            pltpu.SemaphoreType.DMA((5,)),
            pltpu.SemaphoreType.REGULAR,
            pltpu.SemaphoreType.REGULAR,
        ],
        compiler_params=pltpu.CompilerParams(
            collective_id=0, has_side_effects=True, vmem_limit_bytes=32 * 1024 * 1024
        ),
        cost_estimate=pl.CostEstimate(
            flops=2 * 400_000_000, bytes_accessed=2_000_000, transcendentals=100_000
        ),
    )(*[
        pltpu.with_memory_space_constraint(a, pltpu.HBM)
        for a in (
            flat(gate_out),
            flat(gate_in),
            flat(signal),
            flat(cotangent),
            residue.T,
            decay.T,
            skip_bias.reshape(1, channels),
            channel_group.reshape(1, channels),
        )
    ])
    results = pl.pallas_call(
        functools.partial(store_kernel, len(shapes)),
        out_shape=shapes,
        in_specs=[vmem] * len(shapes),
        out_specs=[hbm] * len(shapes),
        scratch_shapes=[pltpu.SemaphoreType.DMA((len(shapes),))],
        compiler_params=pltpu.CompilerParams(vmem_limit_bytes=4 * 1024 * 1024),
    )(*results)
    lifted = tuple(a.reshape(1, channels, rows) for a in results[:4])
    return lifted + (results[4], results[5].T, results[6].reshape(channels))


def solution(mesh):
    return jax.shard_map(
        body,
        mesh=mesh,
        in_specs=(
            P("dp", None, "ctx"),
            P("dp", None, "ctx"),
            P("dp", None, "ctx"),
            P("dp", None, "ctx"),
            P(),
            P(),
            P(),
            P(),
        ),
        out_specs=(
            P("dp", None, "ctx"),
            P("dp", None, "ctx"),
            P("dp", None, "ctx"),
            P("dp", None, "ctx"),
            P(None, "ctx"),
            P(),
            P(),
        ),
        check_vma=False,
    )
```

```python
import functools
import math

import jax
import jax.numpy as jnp
from jax import lax
from jax.experimental import pallas as pl
from jax.experimental.pallas import tpu as pltpu
from jax.sharding import PartitionSpec as P

GROUP_SIZE = 16
PLANE_SEQS = 2
MESH = pl.DeviceIdType.MESH
EXACT = lax.Precision.HIGHEST
F32 = jnp.float32
BF16 = jnp.bfloat16


def iota(shape, dim):
    return lax.broadcasted_iota(jnp.int32, shape, dim)


def matmul(left, right, dims=(1, 0), precision=None):
    return lax.dot_general(
        left,
        right,
        (((dims[0],), (dims[1],)), ((), ())),
        precision=precision,
        preferred_element_type=F32,
    )


def kernel(
    data_size,
    ctx_size,
    gate_out_hbm,
    gate_in_hbm,
    signal_hbm,
    cotangent_hbm,
    residue_hbm,
    decay_hbm,
    skip_bias_hbm,
    channel_group_hbm,
    conv_out,
    grad_gate_out,
    grad_gate_in,
    grad_signal,
    grad_filter,
    grad_residue,
    grad_bias,
    gate_out,
    gate_in,
    signal,
    cotangent,
    residue,
    decay,
    skip_bias,
    channel_group,
    load_sems,
    sorted_in,
    got,
    unsort,
    bias_wide,
    ranks,
    basis,
    taps,
    lags,
    lag_rows,
    term_send,
    term_got,
    small_send,
    small_got,
    back_send,
    back_got,
    sum_send,
    sum_got,
    final,
    send_sems,
    recv_sems,
    plane_ready,
    levels_ready,
):
    modes, groups = residue.shape
    channels, rows = gate_out.shape
    seq_len = rows * ctx_size
    depth = data_size // PLANE_SEQS
    blocks = ctx_size * GROUP_SIZE
    ctx_index = lax.axis_index("ctx")
    plane_seq = lax.axis_index("dp") // depth
    level = lax.axis_index("dp") % depth
    plane_index = plane_seq * ctx_size + ctx_index

    wide_y = ctx_size // 4
    here = (ctx_index // 4, 2 * (lax.rem(ctx_index, 4) // 2) + plane_seq, lax.rem(ctx_index, 2))

    def offset(i):
        return jnp.where(i == 2, 3, jnp.where(i == 3, 0, 2 - i))

    def visit(step, chip, side):
        y = lax.rem(here[0] + offset(chip // 4 + 4 - wide_y), wide_y)
        x = lax.rem(here[1] + offset(lax.rem(chip, 4)), 4)
        rank = 4 * y + 2 * (x // 2) + side
        seq = lax.rem(x, 2)
        step(seq * ctx_size + rank, seq, rank, {"dp": seq * depth + level, "ctx": rank})

    def over_plane(step):
        def one(i, c):
            visit(step, i // 2, lax.rem(here[2] + 1 + i, 2))
            return c

        lax.fori_loop(0, groups - 1, one, 0)

    def over_chips(step, side, count):
        lax.fori_loop(0, count, lambda i, c: (visit(step, i, side), c)[1], 0)

    def over_column(step):
        def one(i, c):
            o = depth // 2 + (i + 1) // 2 * (1 - 2 * lax.rem(i, 2))
            step({"dp": plane_seq * depth + lax.rem(level + o, depth)})
            return c

        lax.fori_loop(0, depth - 1, one, 0)

    def push(src, dst, phase, target):
        pltpu.make_async_remote_copy(
            src_ref=src,
            dst_ref=dst,
            send_sem=send_sems.at[phase],
            recv_sem=recv_sems.at[phase],
            device_id=target,
            device_id_type=MESH,
        ).start()

    def arrived(span, phase):
        pltpu.make_async_copy(span, span, recv_sems.at[phase]).wait()

    def sent(span, phase):
        pltpu.make_async_copy(span, span, send_sems.at[phase]).wait()

    def arrived_plane(phase):
        span = sorted_in.at[pl.ds(0, channels - GROUP_SIZE)]
        arrived(span, phase)

    loads = [
        pltpu.make_async_copy(src, dst, load_sems.at[i])
        for i, (src, dst) in enumerate(
            [
                (channel_group_hbm, channel_group),
                (gate_in_hbm, gate_in),
                (signal_hbm, signal),
                (gate_out_hbm, gate_out),
                (cotangent_hbm, cotangent),
                (decay_hbm, decay),
                (residue_hbm, residue),
                (skip_bias_hbm, skip_bias),
            ]
        )
    ]
    for load in loads:
        load.start()

    barrier = pltpu.get_barrier_semaphore()
    core = lax.rem(ctx_index, 2)
    mate = {"ctx": ctx_index + 1 - 2 * core}

    def greet_plane(p, s, k, target):
        @pl.when(lax.rem(k, 2) == 1)
        def _():
            pl.semaphore_signal(barrier, inc=1, device_id=target, device_id_type=MESH)

    over_plane(greet_plane)
    over_column(
        lambda target: pl.semaphore_signal(
            barrier,
            inc=1,
            device_id={"dp": target["dp"], "ctx": ctx_index - core},
            device_id_type=MESH,
        )
    )

    loads[0].wait()
    member = iota((groups, channels), 0) == channel_group[...]
    before = jnp.where(iota((channels, channels), 0) < iota((channels, channels), 1), 1.0, 0.0)
    rank = matmul(jnp.where(member, 1.0, 0.0).astype(BF16), before.astype(BF16))
    rank = jnp.sum(jnp.where(member, rank, 0.0), axis=0, keepdims=True)
    ranks[...] = rank
    first = jnp.sum(
        jnp.where(member, iota((groups, channels), 0).astype(F32), 0.0), axis=0, keepdims=True
    )
    place = first * GROUP_SIZE + rank
    sort = jnp.where(iota((channels, channels), 0).astype(F32) == place, 1.0, 0.0).astype(BF16)

    for load in loads[1:5]:
        load.wait()
    mixed = (gate_in[...].astype(F32) * signal[...].astype(F32)).astype(BF16)
    back = (cotangent[...].astype(F32) * gate_out[...].astype(F32)).astype(BF16)
    sorted_in[...] = matmul(sort, jnp.concatenate([mixed, back], axis=1)).astype(BF16)

    def channels_of(peer):
        return pl.ds(pl.multiple_of(peer * GROUP_SIZE, GROUP_SIZE), GROUP_SIZE)

    got[plane_seq, ctx_index] = sorted_in[channels_of(plane_index)]

    @pl.when(core == 1)
    def _():
        pl.semaphore_wait(barrier, groups - 1)
        pl.semaphore_signal(plane_ready, inc=1, device_id=mate, device_id_type=MESH)

    @pl.when(core == 0)
    def _():
        pl.semaphore_wait(plane_ready, 1)

    over_plane(
        lambda p, s, k, target: push(
            sorted_in.at[channels_of(p)], got.at[plane_seq, ctx_index], 0, target
        )
    )

    for load in loads[5:]:
        load.wait()
    place_wide = jnp.transpose(jnp.broadcast_to(place, (128, channels)))
    unsort[...] = jnp.where(
        iota((channels, channels), 1).astype(F32) == place_wide[:, :1], 1.0, 0.0
    ).astype(BF16)
    bias_wide[...] = jnp.transpose(jnp.broadcast_to(skip_bias[...], (rows, channels)))
    lane = iota((modes, rows), 1).astype(F32)
    pick = jnp.where(iota((groups, rows), 0) == plane_index, 1.0, 0.0)
    rate = matmul(decay[...], pick, precision=EXACT)
    weight = matmul(residue[...], pick, precision=EXACT)
    for i in range(ctx_size):
        basis[:, i * rows : (i + 1) * rows] = jnp.exp(-rate * ((lane + i * rows) / seq_len))
    filt = matmul(weight * jnp.exp(rate * (lane / seq_len)), basis[...], (0, 0), EXACT)
    causal = iota((rows, rows), 1) >= iota((rows, rows), 0)
    taps[:, :rows] = jnp.zeros((rows, rows), BF16)
    taps[:, rows : 2 * rows] = jnp.where(causal, filt[:, :rows], 0.0).astype(BF16)
    taps[:, 2 * rows :] = filt[:, rows:].astype(BF16)

    @pl.when(core == 0)
    def _():
        pl.semaphore_wait(barrier, 2 * (depth - 1))
        pl.semaphore_signal(levels_ready, inc=1, device_id=mate, device_id_type=MESH)

    arrived_plane(0)

    mixes = [got[s, :, :, :rows].reshape(blocks, rows) for s in range(PLANE_SEQS)]
    grads = [got[s, :, :, rows:].reshape(blocks, rows) for s in range(PLANE_SEQS)]
    mix_t = jnp.transpose(jnp.concatenate(mixes, axis=0))

    def shifted(k):
        if k == 0:
            return jnp.concatenate(grads, axis=0)
        gap = jnp.zeros((k * GROUP_SIZE, rows), BF16)
        return jnp.concatenate([x for a in grads for x in (a[k * GROUP_SIZE :], gap)], axis=0)

    for k in range(0, ctx_size, 2):
        pair = jnp.concatenate([shifted(k), shifted(k + 1)], axis=1)
        lags[:, k * rows : (k + 2) * rows] = matmul(mix_t, pair)
    width = seq_len + rows
    lags[:, seq_len:] = jnp.zeros((rows, rows), F32)
    parts = [lags[a * 8 : (a + 1) * 8, :] for a in range(rows // 8)]
    shift = 8
    while len(parts) > 1:
        parts = [
            parts[a] + pltpu.roll(parts[a + 1], width - shift, 1) for a in range(0, len(parts), 2)
        ]
        shift *= 2
    skew = parts[0]
    row = iota((8, width), 0)
    for bit in (1, 2, 4):
        skew = jnp.where(row & bit != 0, pltpu.roll(skew, width - bit, 1), skew)
    corr = jnp.sum(skew, axis=0, keepdims=True)
    for i in range(ctx_size):
        lag_rows[i : i + 1, :] = corr[:, i * rows : (i + 1) * rows]
    term_send[...] = lag_rows[...].astype(BF16)

    @pl.when(core == 1)
    def _():
        pl.semaphore_wait(levels_ready, 1)

    def to_column(src, dst, phase):
        over_column(
            lambda target: push(
                src, dst, phase, {"dp": target["dp"], "ctx": ctx_index + 1 - core}
            )
        )

        @pl.when(core == 0)
        def _():
            push(src, dst, phase, mate)

    @pl.when(core == 1)
    def _():
        term_got[2 * level + 1] = term_send[...]

    to_column(term_send, term_got.at[2 * level + core], 1)

    modal = jnp.zeros((modes, rows), F32)
    direct = jnp.zeros((GROUP_SIZE, rows), F32)
    for i in range(ctx_size):
        span = slice(i * rows, (i + 1) * rows)
        modal = modal + basis[:, span] * corr[:, span]
        for s in range(PLANE_SEQS):
            direct = direct + got[s, i, :, :rows].astype(F32) * got[s, i, :, rows:].astype(F32)
    stack = jnp.concatenate(
        [modal, direct, jnp.zeros((rows - modes - GROUP_SIZE, rows), F32)], axis=0
    )
    small_send[...] = matmul(jnp.ones((8, rows), F32), stack, (1, 1), EXACT)[:1]

    @pl.when(core == 1)
    def _():
        small_got[2 * level + 1] = small_send[...]

    to_column(small_send, small_got.at[2 * level + core], 4)

    pairs = ctx_size // 2
    wide = [
        jnp.concatenate([got[s, 2 * p], got[s, 2 * p + 1]], axis=1)
        for p in range(pairs)
        for s in range(PLANE_SEQS)
    ]
    wide = jnp.concatenate(wide, axis=0)
    mix = jnp.concatenate([wide[:, :rows], wide[:, 2 * rows : 3 * rows]], axis=1)
    grad = jnp.concatenate([wide[:, rows : 2 * rows], wide[:, 3 * rows :]], axis=1)
    step = PLANE_SEQS * GROUP_SIZE
    state = jnp.zeros((pairs * step, 2 * rows), F32)
    prior = jnp.zeros((pairs * step, 2 * rows), F32)
    for q in range(pairs):
        block = jnp.concatenate(
            [
                taps[:, (2 * q + 1) * rows : (2 * q + 3) * rows],
                taps[:, 2 * q * rows : (2 * q + 2) * rows],
            ],
            axis=0,
        )
        cut = q * step
        ahead = matmul(mix[: pairs * step - cut], block)
        behind = matmul(grad[cut:], block, (1, 1))
        if q == 0:
            state, prior = ahead, behind
        else:
            gap = jnp.zeros((cut, 2 * rows), F32)
            state = state + jnp.concatenate([gap, ahead], axis=0)
            prior = prior + jnp.concatenate([behind, gap], axis=0)
    state = state.astype(BF16)
    prior = prior.astype(BF16)
    for s in range(PLANE_SEQS):
        for i in range(ctx_size):
            first_row = (i // 2) * step + s * GROUP_SIZE
            at = slice(first_row, first_row + GROUP_SIZE)
            span = slice((i % 2) * rows, (i % 2 + 1) * rows)
            back_send[s, i, :, :rows] = state[at, span]
            back_send[s, i, :, rows:] = prior[at, span]
    back_got[channels_of(plane_index)] = back_send[plane_seq, ctx_index]
    over_plane(
        lambda p, s, k, target: push(
            back_send.at[s, k], back_got.at[channels_of(plane_index)], 2, target
        )
    )

    filter_scale = 1.0 / math.sqrt(data_size * seq_len * GROUP_SIZE)
    at = iota((1, rows), 1)
    small_scale = jnp.where(
        at < modes, filter_scale / math.sqrt(seq_len), 1.0 / math.sqrt(data_size * seq_len)
    )
    pair = pl.ds(plane_index - 1, 2)

    @pl.when(core == 1)
    def _():
        arrived(term_got.at[pl.ds(0, 2 * depth - 1)], 1)
        arrived(small_got.at[pl.ds(0, 2 * depth - 1)], 4)
        for c in range(2):
            total = term_got[c].astype(F32)
            small = small_got[c]
            for i in range(1, depth):
                total = total + term_got[2 * i + c].astype(F32)
                small = small + small_got[2 * i + c]
            total = total * filter_scale
            small = small * small_scale
            for i in range(ctx_size):
                sum_send[i, c, :, :rows] = total[i : i + 1]
                sum_send[i, c, :, rows:] = small
        sum_got[pair] = sum_send[ctx_index]

        def push_sums(phase):
            return lambda p, s, k, target: push(
                sum_send.at[k], sum_got.at[pair], phase, target
            )

        over_chips(push_sums(3), 1, groups // 2 - 1)
        over_chips(push_sums(5), 0, groups // 2)

    arrived_plane(2)
    results = matmul(unsort[...], back_got[...])
    wide_gate = gate_out[...].astype(F32)
    wide_cot = cotangent[...].astype(F32)
    wide_in = gate_in[...].astype(F32)
    wide_signal = signal[...].astype(F32)
    mixed_wide = (wide_in * wide_signal).astype(BF16).astype(F32)
    back_wide = (wide_cot * wide_gate).astype(BF16).astype(F32)
    mixture = results[:, :rows] + bias_wide[...] * mixed_wide
    conv_out[...] = (wide_gate * mixture).astype(BF16)
    grad_gate_out[...] = (wide_cot * mixture).astype(BF16)
    grad_mixed = results[:, rows:] + bias_wide[...] * back_wide
    grad_gate_in[...] = (grad_mixed * wide_signal).astype(BF16)
    grad_signal[...] = (grad_mixed * wide_in).astype(BF16)

    @pl.when(core == 0)
    def _():
        arrived(sum_got, 5)

    @pl.when(core == 1)
    def _():
        arrived(sum_got.at[pl.ds(0, groups - 2)], 3)

    for g in range(groups):
        final[g : g + 1, :] = sum_got[g]
    grad_filter[...] = final[:, :rows]
    small = jnp.transpose(final[:, rows:])
    grad_residue[...] = small[:modes]
    terms = small[modes : modes + GROUP_SIZE]
    upper = terms.astype(BF16)
    middle = (terms - upper.astype(F32)).astype(BF16)
    lower = (terms - upper.astype(F32) - middle.astype(F32)).astype(BF16)
    spread = matmul(
        jnp.concatenate([upper, middle, lower], axis=0), jnp.where(member, 1.0, 0.0).astype(BF16)
    )
    spread = (
        spread[:GROUP_SIZE] + spread[GROUP_SIZE : 2 * GROUP_SIZE] + spread[2 * GROUP_SIZE :]
    )
    hit = iota((GROUP_SIZE, channels), 0).astype(F32) == ranks[...]
    grad_bias[...] = jnp.sum(jnp.where(hit, spread, 0.0), axis=0, keepdims=True)

    sent(sorted_in.at[pl.ds(0, channels - GROUP_SIZE)], 0)
    sent(back_got.at[pl.ds(0, channels - GROUP_SIZE)], 2)

    @pl.when(core == 0)
    def _():
        sent(term_got.at[pl.ds(0, depth)], 1)
        sent(small_got.at[pl.ds(0, depth)], 4)

    @pl.when(core == 1)
    def _():
        sent(term_got.at[pl.ds(0, depth - 1)], 1)
        sent(small_got.at[pl.ds(0, depth - 1)], 4)
        sent(sum_send.at[pl.ds(0, groups // 2 - 1)], 3)
        sent(sum_send, 5)


def store_kernel(count, *refs):
    sources, results, sems = refs[:count], refs[count : 2 * count], refs[2 * count]
    stores = [
        pltpu.make_async_copy(src, dst, sems.at[i])
        for i, (src, dst) in enumerate(zip(sources, results))
    ]
    for store in stores:
        store.start()
    for store in stores:
        store.wait()


def body(gate_out, gate_in, signal, cotangent, residue, decay, skip_bias, channel_group):
    data_size = lax.axis_size("dp")
    ctx_size = lax.axis_size("ctx")
    _, channels, rows = gate_out.shape
    groups, modes = residue.shape
    depth = data_size // PLANE_SEQS
    seq_len = rows * ctx_size
    vmem = pl.BlockSpec(memory_space=pltpu.VMEM)
    hbm = pl.BlockSpec(memory_space=pltpu.HBM)
    wide = jax.ShapeDtypeStruct((channels, rows), BF16)
    flat = lambda a: a.reshape(channels, rows)
    shapes = [
        wide,
        wide,
        wide,
        wide,
        jax.ShapeDtypeStruct((groups, rows), F32),
        jax.ShapeDtypeStruct((modes, groups), F32),
        jax.ShapeDtypeStruct((1, channels), F32),
    ]
    results = pl.pallas_call(
        functools.partial(kernel, data_size, ctx_size),
        out_shape=[pltpu.VMEM(a.shape, a.dtype) for a in shapes],
        in_specs=[hbm] * 8,
        out_specs=[vmem] * len(shapes),
        scratch_shapes=[
            pltpu.VMEM((channels, rows), BF16),
            pltpu.VMEM((channels, rows), BF16),
            pltpu.VMEM((channels, rows), BF16),
            pltpu.VMEM((channels, rows), BF16),
            pltpu.VMEM((modes, groups), F32),
            pltpu.VMEM((modes, groups), F32),
            pltpu.VMEM((1, channels), F32),
            pltpu.VMEM((1, channels), jnp.int32),
            pltpu.SemaphoreType.DMA((8,)),
            pltpu.VMEM((channels, 2 * rows), BF16),
            pltpu.VMEM((PLANE_SEQS, ctx_size, GROUP_SIZE, 2 * rows), BF16),
            pltpu.VMEM((channels, channels), BF16),
            pltpu.VMEM((channels, rows), F32),
            pltpu.VMEM((1, channels), F32),
            pltpu.VMEM((modes, seq_len), F32),
            pltpu.VMEM((rows, seq_len + rows), BF16),
            pltpu.VMEM((rows, seq_len + rows), F32),
            pltpu.VMEM((ctx_size, rows), F32),
            pltpu.VMEM((ctx_size, rows), BF16),
            pltpu.VMEM((2 * depth, ctx_size, rows), BF16),
            pltpu.VMEM((1, rows), F32),
            pltpu.VMEM((2 * depth, 1, rows), F32),
            pltpu.VMEM((PLANE_SEQS, ctx_size, GROUP_SIZE, 2 * rows), BF16),
            pltpu.VMEM((channels, 2 * rows), BF16),
            pltpu.VMEM((ctx_size, 2, 1, 2 * rows), F32),
            pltpu.VMEM((groups, 1, 2 * rows), F32),
            pltpu.VMEM((groups, 2 * rows), F32),
            pltpu.SemaphoreType.DMA((6,)),
            pltpu.SemaphoreType.DMA((6,)),
            pltpu.SemaphoreType.REGULAR,
            pltpu.SemaphoreType.REGULAR,
        ],
        compiler_params=pltpu.CompilerParams(
            collective_id=0, has_side_effects=True, vmem_limit_bytes=32 * 1024 * 1024
        ),
        cost_estimate=pl.CostEstimate(
            flops=2 * 400_000_000, bytes_accessed=2_000_000, transcendentals=100_000
        ),
    )(*[
        pltpu.with_memory_space_constraint(a, pltpu.HBM)
        for a in (
            flat(gate_out),
            flat(gate_in),
            flat(signal),
            flat(cotangent),
            residue.T,
            decay.T,
            skip_bias.reshape(1, channels),
            channel_group.reshape(1, channels),
        )
    ])
    results = pl.pallas_call(
        functools.partial(store_kernel, len(shapes)),
        out_shape=shapes,
        in_specs=[vmem] * len(shapes),
        out_specs=[hbm] * len(shapes),
        scratch_shapes=[pltpu.SemaphoreType.DMA((len(shapes),))],
        compiler_params=pltpu.CompilerParams(vmem_limit_bytes=4 * 1024 * 1024),
    )(*results)
    lifted = tuple(a.reshape(1, channels, rows) for a in results[:4])
    return lifted + (results[4], results[5].T, results[6].reshape(channels))


def solution(mesh):
    return jax.shard_map(
        body,
        mesh=mesh,
        in_specs=(
            P("dp", None, "ctx"),
            P("dp", None, "ctx"),
            P("dp", None, "ctx"),
            P("dp", None, "ctx"),
            P(),
            P(),
            P(),
            P(),
        ),
        out_specs=(
            P("dp", None, "ctx"),
            P("dp", None, "ctx"),
            P("dp", None, "ctx"),
            P("dp", None, "ctx"),
            P(None, "ctx"),
            P(),
            P(),
        ),
        check_vma=False,
    )
```

```python
import functools
import math

import jax
import jax.numpy as jnp
from jax import lax
from jax.experimental import pallas as pl
from jax.experimental.pallas import tpu as pltpu
from jax.sharding import PartitionSpec as P

GROUP_SIZE = 16
PLANE_SEQS = 2
MESH = pl.DeviceIdType.MESH
EXACT = lax.Precision.HIGHEST
F32 = jnp.float32
BF16 = jnp.bfloat16


def iota(shape, dim):
    return lax.broadcasted_iota(jnp.int32, shape, dim)


def matmul(left, right, dims=(1, 0), precision=None):
    return lax.dot_general(
        left,
        right,
        (((dims[0],), (dims[1],)), ((), ())),
        precision=precision,
        preferred_element_type=F32,
    )


def kernel(
    data_size,
    ctx_size,
    gate_out_hbm,
    gate_in_hbm,
    signal_hbm,
    cotangent_hbm,
    residue_hbm,
    decay_hbm,
    skip_bias_hbm,
    channel_group_hbm,
    conv_out,
    grad_gate_out,
    grad_gate_in,
    grad_signal,
    grad_filter,
    grad_residue,
    grad_bias,
    gate_out,
    gate_in,
    signal,
    cotangent,
    residue,
    decay,
    skip_bias,
    channel_group,
    load_sems,
    sorted_in,
    got,
    unsort,
    bias_wide,
    ranks,
    basis,
    taps,
    lags,
    lag_rows,
    term_send,
    term_got,
    small_send,
    small_got,
    back_send,
    back_got,
    sum_send,
    sum_got,
    final,
    send_sems,
    recv_sems,
    plane_ready,
    levels_ready,
):
    modes, groups = residue.shape
    channels, rows = gate_out.shape
    seq_len = rows * ctx_size
    depth = data_size // PLANE_SEQS
    blocks = ctx_size * GROUP_SIZE
    ctx_index = lax.axis_index("ctx")
    plane_seq = lax.axis_index("dp") // depth
    level = lax.axis_index("dp") % depth
    plane_index = plane_seq * ctx_size + ctx_index

    wide_y = ctx_size // 4
    core = lax.rem(ctx_index, 2)
    here_y = ctx_index // 4
    here_x = 2 * (lax.rem(ctx_index, 4) // 2) + plane_seq
    chips = []
    for dy in (2, 1, 3, 0)[4 - wide_y :]:
        y = lax.rem(here_y + dy, wide_y)
        for dx in (2, 1, 3, 0):
            x = lax.rem(here_x + dx, 4)
            seq = lax.rem(x, 2)
            chips.append((4 * y + x - seq, seq, seq * depth + level))
    half = depth // 2
    column = [half + (i + 1) // 2 * (1 - 2 * (i % 2)) for i in range(depth - 1)]
    column = [plane_seq * depth + lax.rem(level + o, depth) for o in column]

    def visit(step, chip, side):
        first, seq, data_rank = chip
        rank = first + side
        step(seq * ctx_size + rank, seq, rank, {"dp": data_rank, "ctx": rank})

    def over_plane(step):
        for chip in chips[:-1]:
            visit(step, chip, 1 - core)
            visit(step, chip, core)
        visit(step, chips[-1], 1 - core)

    def over_chips(step, side, count):
        for chip in chips[:count]:
            visit(step, chip, side)

    def over_column(step):
        for data_rank in column:
            step({"dp": data_rank})

    def push(src, dst, phase, target):
        pltpu.make_async_remote_copy(
            src_ref=src,
            dst_ref=dst,
            send_sem=send_sems.at[phase],
            recv_sem=recv_sems.at[phase],
            device_id=target,
            device_id_type=MESH,
        ).start()

    def arrived(span, phase):
        pltpu.make_async_copy(span, span, recv_sems.at[phase]).wait()

    def sent(span, phase):
        pltpu.make_async_copy(span, span, send_sems.at[phase]).wait()

    def arrived_plane(phase):
        span = sorted_in.at[pl.ds(0, channels - GROUP_SIZE)]
        arrived(span, phase)

    loads = [
        pltpu.make_async_copy(src, dst, load_sems.at[i])
        for i, (src, dst) in enumerate(
            [
                (channel_group_hbm, channel_group),
                (gate_in_hbm, gate_in),
                (signal_hbm, signal),
                (gate_out_hbm, gate_out),
                (cotangent_hbm, cotangent),
                (decay_hbm, decay),
                (residue_hbm, residue),
                (skip_bias_hbm, skip_bias),
            ]
        )
    ]
    for load in loads:
        load.start()

    barrier = pltpu.get_barrier_semaphore()
    mate = {"ctx": ctx_index + 1 - 2 * core}

    def greet(p, s, k, target):
        pl.semaphore_signal(barrier, inc=1, device_id=target, device_id_type=MESH)

    over_chips(greet, 1, groups // 2 - 1)

    @pl.when(core == 0)
    def _():
        pl.semaphore_signal(barrier, inc=1, device_id=mate, device_id_type=MESH)

    over_column(
        lambda target: pl.semaphore_signal(
            barrier,
            inc=1,
            device_id={"dp": target["dp"], "ctx": ctx_index - core},
            device_id_type=MESH,
        )
    )

    loads[0].wait()
    member = iota((groups, channels), 0) == channel_group[...]
    before = jnp.where(iota((channels, channels), 0) < iota((channels, channels), 1), 1.0, 0.0)
    rank = matmul(jnp.where(member, 1.0, 0.0).astype(BF16), before.astype(BF16))
    rank = jnp.sum(jnp.where(member, rank, 0.0), axis=0, keepdims=True)
    ranks[...] = rank
    first = jnp.sum(
        jnp.where(member, iota((groups, channels), 0).astype(F32), 0.0), axis=0, keepdims=True
    )
    place = first * GROUP_SIZE + rank
    sort = jnp.where(iota((channels, channels), 0).astype(F32) == place, 1.0, 0.0).astype(BF16)

    for load in loads[1:5]:
        load.wait()
    mixed = (gate_in[...].astype(F32) * signal[...].astype(F32)).astype(BF16)
    back = (cotangent[...].astype(F32) * gate_out[...].astype(F32)).astype(BF16)
    sorted_in[...] = matmul(sort, jnp.concatenate([mixed, back], axis=1)).astype(BF16)

    def channels_of(peer):
        return pl.ds(pl.multiple_of(peer * GROUP_SIZE, GROUP_SIZE), GROUP_SIZE)

    got[plane_seq, ctx_index] = sorted_in[channels_of(plane_index)]

    @pl.when(core == 1)
    def _():
        pl.semaphore_wait(barrier, groups - 1)
        pl.semaphore_signal(plane_ready, inc=1, device_id=mate, device_id_type=MESH)

    @pl.when(core == 0)
    def _():
        pl.semaphore_wait(plane_ready, 1)

    over_plane(
        lambda p, s, k, target: push(
            sorted_in.at[channels_of(p)], got.at[plane_seq, ctx_index], 0, target
        )
    )

    for load in loads[5:]:
        load.wait()
    place_wide = jnp.transpose(jnp.broadcast_to(place, (128, channels)))
    unsort[...] = jnp.where(
        iota((channels, channels), 1).astype(F32) == place_wide[:, :1], 1.0, 0.0
    ).astype(BF16)
    bias_wide[...] = jnp.transpose(jnp.broadcast_to(skip_bias[...], (rows, channels)))
    lane = iota((modes, rows), 1).astype(F32)
    pick = jnp.where(iota((groups, rows), 0) == plane_index, 1.0, 0.0)
    rate = matmul(decay[...], pick, precision=EXACT)
    weight = matmul(residue[...], pick, precision=EXACT)
    for i in range(ctx_size):
        basis[:, i * rows : (i + 1) * rows] = jnp.exp(-rate * ((lane + i * rows) / seq_len))
    filt = matmul(weight * jnp.exp(rate * (lane / seq_len)), basis[...], (0, 0), EXACT)
    causal = iota((rows, rows), 1) >= iota((rows, rows), 0)
    taps[:, :rows] = jnp.zeros((rows, rows), BF16)
    taps[:, rows : 2 * rows] = jnp.where(causal, filt[:, :rows], 0.0).astype(BF16)
    taps[:, 2 * rows :] = filt[:, rows:].astype(BF16)

    @pl.when(core == 0)
    def _():
        pl.semaphore_wait(barrier, 2 * (depth - 1))
        pl.semaphore_signal(levels_ready, inc=1, device_id=mate, device_id_type=MESH)

    arrived_plane(0)

    mixes = [got[s, :, :, :rows].reshape(blocks, rows) for s in range(PLANE_SEQS)]
    grads = [got[s, :, :, rows:].reshape(blocks, rows) for s in range(PLANE_SEQS)]
    mix_t = jnp.transpose(jnp.concatenate(mixes, axis=0))

    def shifted(k):
        if k == 0:
            return jnp.concatenate(grads, axis=0)
        gap = jnp.zeros((k * GROUP_SIZE, rows), BF16)
        return jnp.concatenate([x for a in grads for x in (a[k * GROUP_SIZE :], gap)], axis=0)

    for k in range(0, ctx_size, 2):
        pair = jnp.concatenate([shifted(k), shifted(k + 1)], axis=1)
        lags[:, k * rows : (k + 2) * rows] = matmul(mix_t, pair)
    width = seq_len + rows
    lags[:, seq_len:] = jnp.zeros((rows, rows), F32)
    parts = [lags[a * 8 : (a + 1) * 8, :] for a in range(rows // 8)]
    shift = 8
    while len(parts) > 1:
        parts = [
            parts[a] + pltpu.roll(parts[a + 1], width - shift, 1) for a in range(0, len(parts), 2)
        ]
        shift *= 2
    skew = parts[0]
    row = iota((8, width), 0)
    for bit in (1, 2, 4):
        skew = jnp.where(row & bit != 0, pltpu.roll(skew, width - bit, 1), skew)
    corr = jnp.sum(skew, axis=0, keepdims=True)
    for i in range(ctx_size):
        lag_rows[i : i + 1, :] = corr[:, i * rows : (i + 1) * rows]
    term_send[...] = lag_rows[...].astype(BF16)

    @pl.when(core == 1)
    def _():
        pl.semaphore_wait(levels_ready, 1)

    def to_column(src, dst, phase):
        over_column(
            lambda target: push(
                src, dst, phase, {"dp": target["dp"], "ctx": ctx_index + 1 - core}
            )
        )

        @pl.when(core == 0)
        def _():
            push(src, dst, phase, mate)

    @pl.when(core == 1)
    def _():
        term_got[2 * level + 1] = term_send[...]

    to_column(term_send, term_got.at[2 * level + core], 1)

    modal = jnp.zeros((modes, rows), F32)
    direct = jnp.zeros((GROUP_SIZE, rows), F32)
    for i in range(ctx_size):
        span = slice(i * rows, (i + 1) * rows)
        modal = modal + basis[:, span] * corr[:, span]
        for s in range(PLANE_SEQS):
            direct = direct + got[s, i, :, :rows].astype(F32) * got[s, i, :, rows:].astype(F32)
    stack = jnp.concatenate(
        [modal, direct, jnp.zeros((rows - modes - GROUP_SIZE, rows), F32)], axis=0
    )
    small_send[...] = matmul(jnp.ones((8, rows), F32), stack, (1, 1), EXACT)[:1]

    @pl.when(core == 1)
    def _():
        small_got[2 * level + 1] = small_send[...]

    to_column(small_send, small_got.at[2 * level + core], 4)

    pairs = ctx_size // 2
    wide = [
        jnp.concatenate([got[s, 2 * p], got[s, 2 * p + 1]], axis=1)
        for p in range(pairs)
        for s in range(PLANE_SEQS)
    ]
    wide = jnp.concatenate(wide, axis=0)
    mix = jnp.concatenate([wide[:, :rows], wide[:, 2 * rows : 3 * rows]], axis=1)
    grad = jnp.concatenate([wide[:, rows : 2 * rows], wide[:, 3 * rows :]], axis=1)
    step = PLANE_SEQS * GROUP_SIZE
    state = jnp.zeros((pairs * step, 2 * rows), F32)
    prior = jnp.zeros((pairs * step, 2 * rows), F32)
    for q in range(pairs):
        block = jnp.concatenate(
            [
                taps[:, (2 * q + 1) * rows : (2 * q + 3) * rows],
                taps[:, 2 * q * rows : (2 * q + 2) * rows],
            ],
            axis=0,
        )
        cut = q * step
        ahead = matmul(mix[: pairs * step - cut], block)
        behind = matmul(grad[cut:], block, (1, 1))
        if q == 0:
            state, prior = ahead, behind
        else:
            gap = jnp.zeros((cut, 2 * rows), F32)
            state = state + jnp.concatenate([gap, ahead], axis=0)
            prior = prior + jnp.concatenate([behind, gap], axis=0)
    state = state.astype(BF16)
    prior = prior.astype(BF16)
    for s in range(PLANE_SEQS):
        for i in range(ctx_size):
            first_row = (i // 2) * step + s * GROUP_SIZE
            at = slice(first_row, first_row + GROUP_SIZE)
            span = slice((i % 2) * rows, (i % 2 + 1) * rows)
            back_send[s, i, :, :rows] = state[at, span]
            back_send[s, i, :, rows:] = prior[at, span]
    back_got[channels_of(plane_index)] = back_send[plane_seq, ctx_index]
    over_plane(
        lambda p, s, k, target: push(
            back_send.at[s, k], back_got.at[channels_of(plane_index)], 2, target
        )
    )

    filter_scale = 1.0 / math.sqrt(data_size * seq_len * GROUP_SIZE)
    at = iota((1, rows), 1)
    small_scale = jnp.where(
        at < modes, filter_scale / math.sqrt(seq_len), 1.0 / math.sqrt(data_size * seq_len)
    )
    pair = pl.ds(plane_index - 1, 2)

    @pl.when(core == 1)
    def _():
        arrived(term_got.at[pl.ds(0, 2 * depth - 1)], 1)
        arrived(small_got.at[pl.ds(0, 2 * depth - 1)], 4)
        for c in range(2):
            total = term_got[c].astype(F32)
            small = small_got[c]
            for i in range(1, depth):
                total = total + term_got[2 * i + c].astype(F32)
                small = small + small_got[2 * i + c]
            total = total * filter_scale
            small = small * small_scale
            for i in range(ctx_size):
                sum_send[i, c, :, :rows] = total[i : i + 1]
                sum_send[i, c, :, rows:] = small
        sum_got[pair] = sum_send[ctx_index]

        def push_sums(phase):
            return lambda p, s, k, target: push(
                sum_send.at[k], sum_got.at[pair], phase, target
            )

        over_chips(push_sums(3), 1, groups // 2 - 1)
        over_chips(push_sums(5), 0, groups // 2)

    arrived_plane(2)
    results = matmul(unsort[...], back_got[...])
    wide_gate = gate_out[...].astype(F32)
    wide_cot = cotangent[...].astype(F32)
    wide_in = gate_in[...].astype(F32)
    wide_signal = signal[...].astype(F32)
    mixed_wide = (wide_in * wide_signal).astype(BF16).astype(F32)
    back_wide = (wide_cot * wide_gate).astype(BF16).astype(F32)
    mixture = results[:, :rows] + bias_wide[...] * mixed_wide
    conv_out[...] = (wide_gate * mixture).astype(BF16)
    grad_gate_out[...] = (wide_cot * mixture).astype(BF16)
    grad_mixed = results[:, rows:] + bias_wide[...] * back_wide
    grad_gate_in[...] = (grad_mixed * wide_signal).astype(BF16)
    grad_signal[...] = (grad_mixed * wide_in).astype(BF16)

    @pl.when(core == 0)
    def _():
        arrived(sum_got, 5)

    @pl.when(core == 1)
    def _():
        arrived(sum_got.at[pl.ds(0, groups - 2)], 3)

    for g in range(groups):
        final[g : g + 1, :] = sum_got[g]
    grad_filter[...] = final[:, :rows]
    small = jnp.transpose(final[:, rows:])
    grad_residue[...] = small[:modes]
    terms = small[modes : modes + GROUP_SIZE]
    upper = terms.astype(BF16)
    middle = (terms - upper.astype(F32)).astype(BF16)
    lower = (terms - upper.astype(F32) - middle.astype(F32)).astype(BF16)
    spread = matmul(
        jnp.concatenate([upper, middle, lower], axis=0), jnp.where(member, 1.0, 0.0).astype(BF16)
    )
    spread = (
        spread[:GROUP_SIZE] + spread[GROUP_SIZE : 2 * GROUP_SIZE] + spread[2 * GROUP_SIZE :]
    )
    hit = iota((GROUP_SIZE, channels), 0).astype(F32) == ranks[...]
    grad_bias[...] = jnp.sum(jnp.where(hit, spread, 0.0), axis=0, keepdims=True)

    sent(sorted_in.at[pl.ds(0, channels - GROUP_SIZE)], 0)
    sent(back_got.at[pl.ds(0, channels - GROUP_SIZE)], 2)

    @pl.when(core == 0)
    def _():
        sent(term_got.at[pl.ds(0, depth)], 1)
        sent(small_got.at[pl.ds(0, depth)], 4)

    @pl.when(core == 1)
    def _():
        sent(term_got.at[pl.ds(0, depth - 1)], 1)
        sent(small_got.at[pl.ds(0, depth - 1)], 4)
        sent(sum_send.at[pl.ds(0, groups // 2 - 1)], 3)
        sent(sum_send, 5)


def store_kernel(count, *refs):
    sources, results, sems = refs[:count], refs[count : 2 * count], refs[2 * count]
    stores = [
        pltpu.make_async_copy(src, dst, sems.at[i])
        for i, (src, dst) in enumerate(zip(sources, results))
    ]
    for store in stores:
        store.start()
    for store in stores:
        store.wait()


def body(gate_out, gate_in, signal, cotangent, residue, decay, skip_bias, channel_group):
    data_size = lax.axis_size("dp")
    ctx_size = lax.axis_size("ctx")
    _, channels, rows = gate_out.shape
    groups, modes = residue.shape
    depth = data_size // PLANE_SEQS
    seq_len = rows * ctx_size
    vmem = pl.BlockSpec(memory_space=pltpu.VMEM)
    hbm = pl.BlockSpec(memory_space=pltpu.HBM)
    wide = jax.ShapeDtypeStruct((channels, rows), BF16)
    flat = lambda a: a.reshape(channels, rows)
    shapes = [
        wide,
        wide,
        wide,
        wide,
        jax.ShapeDtypeStruct((groups, rows), F32),
        jax.ShapeDtypeStruct((modes, groups), F32),
        jax.ShapeDtypeStruct((1, channels), F32),
    ]
    results = pl.pallas_call(
        functools.partial(kernel, data_size, ctx_size),
        out_shape=[pltpu.VMEM(a.shape, a.dtype) for a in shapes],
        in_specs=[hbm] * 8,
        out_specs=[vmem] * len(shapes),
        scratch_shapes=[
            pltpu.VMEM((channels, rows), BF16),
            pltpu.VMEM((channels, rows), BF16),
            pltpu.VMEM((channels, rows), BF16),
            pltpu.VMEM((channels, rows), BF16),
            pltpu.VMEM((modes, groups), F32),
            pltpu.VMEM((modes, groups), F32),
            pltpu.VMEM((1, channels), F32),
            pltpu.VMEM((1, channels), jnp.int32),
            pltpu.SemaphoreType.DMA((8,)),
            pltpu.VMEM((channels, 2 * rows), BF16),
            pltpu.VMEM((PLANE_SEQS, ctx_size, GROUP_SIZE, 2 * rows), BF16),
            pltpu.VMEM((channels, channels), BF16),
            pltpu.VMEM((channels, rows), F32),
            pltpu.VMEM((1, channels), F32),
            pltpu.VMEM((modes, seq_len), F32),
            pltpu.VMEM((rows, seq_len + rows), BF16),
            pltpu.VMEM((rows, seq_len + rows), F32),
            pltpu.VMEM((ctx_size, rows), F32),
            pltpu.VMEM((ctx_size, rows), BF16),
            pltpu.VMEM((2 * depth, ctx_size, rows), BF16),
            pltpu.VMEM((1, rows), F32),
            pltpu.VMEM((2 * depth, 1, rows), F32),
            pltpu.VMEM((PLANE_SEQS, ctx_size, GROUP_SIZE, 2 * rows), BF16),
            pltpu.VMEM((channels, 2 * rows), BF16),
            pltpu.VMEM((ctx_size, 2, 1, 2 * rows), F32),
            pltpu.VMEM((groups, 1, 2 * rows), F32),
            pltpu.VMEM((groups, 2 * rows), F32),
            pltpu.SemaphoreType.DMA((6,)),
            pltpu.SemaphoreType.DMA((6,)),
            pltpu.SemaphoreType.REGULAR,
            pltpu.SemaphoreType.REGULAR,
        ],
        compiler_params=pltpu.CompilerParams(
            collective_id=0, has_side_effects=True, vmem_limit_bytes=32 * 1024 * 1024
        ),
        cost_estimate=pl.CostEstimate(
            flops=2 * 400_000_000, bytes_accessed=2_000_000, transcendentals=100_000
        ),
    )(*[
        pltpu.with_memory_space_constraint(a, pltpu.HBM)
        for a in (
            flat(gate_out),
            flat(gate_in),
            flat(signal),
            flat(cotangent),
            residue.T,
            decay.T,
            skip_bias.reshape(1, channels),
            channel_group.reshape(1, channels),
        )
    ])
    results = pl.pallas_call(
        functools.partial(store_kernel, len(shapes)),
        out_shape=shapes,
        in_specs=[vmem] * len(shapes),
        out_specs=[hbm] * len(shapes),
        scratch_shapes=[pltpu.SemaphoreType.DMA((len(shapes),))],
        compiler_params=pltpu.CompilerParams(vmem_limit_bytes=4 * 1024 * 1024),
    )(*results)
    lifted = tuple(a.reshape(1, channels, rows) for a in results[:4])
    return lifted + (results[4], results[5].T, results[6].reshape(channels))


def solution(mesh):
    return jax.shard_map(
        body,
        mesh=mesh,
        in_specs=(
            P("dp", None, "ctx"),
            P("dp", None, "ctx"),
            P("dp", None, "ctx"),
            P("dp", None, "ctx"),
            P(),
            P(),
            P(),
            P(),
        ),
        out_specs=(
            P("dp", None, "ctx"),
            P("dp", None, "ctx"),
            P("dp", None, "ctx"),
            P("dp", None, "ctx"),
            P(None, "ctx"),
            P(),
            P(),
        ),
        check_vma=False,
    )
```

```python
import functools
import math

import jax
import jax.numpy as jnp
from jax import lax
from jax.experimental import pallas as pl
from jax.experimental.pallas import tpu as pltpu
from jax.sharding import PartitionSpec as P

GROUP_SIZE = 16
PLANE_SEQS = 2
MESH = pl.DeviceIdType.MESH
EXACT = lax.Precision.HIGHEST
F32 = jnp.float32
BF16 = jnp.bfloat16


def iota(shape, dim):
    return lax.broadcasted_iota(jnp.int32, shape, dim)


def matmul(left, right, dims=(1, 0), precision=None):
    return lax.dot_general(
        left,
        right,
        (((dims[0],), (dims[1],)), ((), ())),
        precision=precision,
        preferred_element_type=F32,
    )


def kernel(
    data_size,
    ctx_size,
    gate_out_hbm,
    gate_in_hbm,
    signal_hbm,
    cotangent_hbm,
    residue_hbm,
    decay_hbm,
    skip_bias_hbm,
    channel_group_hbm,
    conv_out,
    grad_gate_out,
    grad_gate_in,
    grad_signal,
    grad_filter,
    grad_residue,
    grad_bias,
    gate_out,
    gate_in,
    signal,
    cotangent,
    residue,
    decay,
    skip_bias,
    channel_group,
    load_sems,
    sorted_in,
    got,
    unsort,
    bias_wide,
    ranks,
    basis,
    taps,
    lags,
    lag_rows,
    term_send,
    term_got,
    small_send,
    small_got,
    back_send,
    back_got,
    sum_send,
    sum_got,
    final,
    send_sems,
    recv_sems,
    plane_ready,
    levels_ready,
):
    modes, groups = residue.shape
    channels, rows = gate_out.shape
    seq_len = rows * ctx_size
    depth = data_size // PLANE_SEQS
    blocks = ctx_size * GROUP_SIZE
    ctx_index = lax.axis_index("ctx")
    plane_seq = lax.axis_index("dp") // depth
    level = lax.axis_index("dp") % depth
    plane_index = plane_seq * ctx_size + ctx_index

    wide_y = ctx_size // 4
    core = lax.rem(ctx_index, 2)
    here_y = ctx_index // 4
    here_x = 2 * (lax.rem(ctx_index, 4) // 2) + plane_seq
    chips = []
    for dy in (2, 1, 3, 0)[4 - wide_y :]:
        y = lax.rem(here_y + dy, wide_y)
        for dx in (2, 1, 3, 0):
            x = lax.rem(here_x + dx, 4)
            seq = lax.rem(x, 2)
            chips.append((4 * y + x - seq, seq, seq * depth + level))
    half = depth // 2
    column = [half + (i + 1) // 2 * (1 - 2 * (i % 2)) for i in range(depth - 1)]
    column = [plane_seq * depth + lax.rem(level + o, depth) for o in column]

    def visit(step, chip, side):
        first, seq, data_rank = chip
        rank = first + side
        step(seq * ctx_size + rank, seq, rank, {"dp": data_rank, "ctx": rank})

    def over_plane(step):
        for chip in chips[:-1]:
            visit(step, chip, 1 - core)
            visit(step, chip, core)
        visit(step, chips[-1], 1 - core)

    def over_chips(step, side, count):
        for chip in chips[:count]:
            visit(step, chip, side)

    def over_column(step):
        for data_rank in column:
            step({"dp": data_rank})

    def push(src, dst, phase, target):
        pltpu.make_async_remote_copy(
            src_ref=src,
            dst_ref=dst,
            send_sem=send_sems.at[phase],
            recv_sem=recv_sems.at[phase],
            device_id=target,
            device_id_type=MESH,
        ).start()

    def arrived(span, phase):
        pltpu.make_async_copy(span, span, recv_sems.at[phase]).wait()

    def sent(span, phase):
        pltpu.make_async_copy(span, span, send_sems.at[phase]).wait()

    def arrived_plane(phase):
        span = sorted_in.at[pl.ds(0, channels - GROUP_SIZE)]
        arrived(span, phase)

    loads = [
        pltpu.make_async_copy(src, dst, load_sems.at[i])
        for i, (src, dst) in enumerate(
            [
                (channel_group_hbm, channel_group),
                (gate_in_hbm, gate_in),
                (signal_hbm, signal),
                (gate_out_hbm, gate_out),
                (cotangent_hbm, cotangent),
                (decay_hbm, decay),
                (residue_hbm, residue),
                (skip_bias_hbm, skip_bias),
            ]
        )
    ]

    barrier = pltpu.get_barrier_semaphore()
    mate = {"ctx": ctx_index + 1 - 2 * core}

    def greet(p, s, k, target):
        pl.semaphore_signal(barrier, inc=1, device_id=target, device_id_type=MESH)

    over_chips(greet, 1, groups // 2 - 1)

    @pl.when(core == 0)
    def _():
        pl.semaphore_signal(barrier, inc=1, device_id=mate, device_id_type=MESH)

    for load in loads:
        load.start()

    over_column(
        lambda target: pl.semaphore_signal(
            barrier,
            inc=1,
            device_id={"dp": target["dp"], "ctx": ctx_index - core},
            device_id_type=MESH,
        )
    )

    loads[0].wait()
    member = iota((groups, channels), 0) == channel_group[...]
    before = jnp.where(iota((channels, channels), 0) < iota((channels, channels), 1), 1.0, 0.0)
    rank = matmul(jnp.where(member, 1.0, 0.0).astype(BF16), before.astype(BF16))
    rank = jnp.sum(jnp.where(member, rank, 0.0), axis=0, keepdims=True)
    ranks[...] = rank
    first = jnp.sum(
        jnp.where(member, iota((groups, channels), 0).astype(F32), 0.0), axis=0, keepdims=True
    )
    place = first * GROUP_SIZE + rank
    sort = jnp.where(iota((channels, channels), 0).astype(F32) == place, 1.0, 0.0).astype(BF16)

    for load in loads[1:5]:
        load.wait()
    mixed = (gate_in[...].astype(F32) * signal[...].astype(F32)).astype(BF16)
    back = (cotangent[...].astype(F32) * gate_out[...].astype(F32)).astype(BF16)
    sorted_in[...] = matmul(sort, jnp.concatenate([mixed, back], axis=1)).astype(BF16)

    def channels_of(peer):
        return pl.ds(pl.multiple_of(peer * GROUP_SIZE, GROUP_SIZE), GROUP_SIZE)

    got[plane_seq, ctx_index] = sorted_in[channels_of(plane_index)]

    @pl.when(core == 1)
    def _():
        pl.semaphore_wait(barrier, groups - 1)
        pl.semaphore_signal(plane_ready, inc=1, device_id=mate, device_id_type=MESH)

    @pl.when(core == 0)
    def _():
        pl.semaphore_wait(plane_ready, 1)

    over_plane(
        lambda p, s, k, target: push(
            sorted_in.at[channels_of(p)], got.at[plane_seq, ctx_index], 0, target
        )
    )

    for load in loads[5:]:
        load.wait()
    place_wide = jnp.transpose(jnp.broadcast_to(place, (128, channels)))
    unsort[...] = jnp.where(
        iota((channels, channels), 1).astype(F32) == place_wide[:, :1], 1.0, 0.0
    ).astype(BF16)
    bias_wide[...] = jnp.transpose(jnp.broadcast_to(skip_bias[...], (rows, channels)))
    lane = iota((modes, rows), 1).astype(F32)
    pick = jnp.where(iota((groups, rows), 0) == plane_index, 1.0, 0.0)
    rate = matmul(decay[...], pick, precision=EXACT)
    weight = matmul(residue[...], pick, precision=EXACT)
    for i in range(ctx_size):
        basis[:, i * rows : (i + 1) * rows] = jnp.exp(-rate * ((lane + i * rows) / seq_len))
    filt = matmul(weight * jnp.exp(rate * (lane / seq_len)), basis[...], (0, 0), EXACT)
    causal = iota((rows, rows), 1) >= iota((rows, rows), 0)
    taps[:, :rows] = jnp.zeros((rows, rows), BF16)
    taps[:, rows : 2 * rows] = jnp.where(causal, filt[:, :rows], 0.0).astype(BF16)
    taps[:, 2 * rows :] = filt[:, rows:].astype(BF16)

    @pl.when(core == 0)
    def _():
        pl.semaphore_wait(barrier, 2 * (depth - 1))
        pl.semaphore_signal(levels_ready, inc=1, device_id=mate, device_id_type=MESH)

    arrived_plane(0)

    mixes = [got[s, :, :, :rows].reshape(blocks, rows) for s in range(PLANE_SEQS)]
    grads = [got[s, :, :, rows:].reshape(blocks, rows) for s in range(PLANE_SEQS)]
    mix_t = jnp.transpose(jnp.concatenate(mixes, axis=0))

    def shifted(k):
        if k == 0:
            return jnp.concatenate(grads, axis=0)
        gap = jnp.zeros((k * GROUP_SIZE, rows), BF16)
        return jnp.concatenate([x for a in grads for x in (a[k * GROUP_SIZE :], gap)], axis=0)

    for k in range(0, ctx_size, 2):
        pair = jnp.concatenate([shifted(k), shifted(k + 1)], axis=1)
        lags[:, k * rows : (k + 2) * rows] = matmul(mix_t, pair)
    width = seq_len + rows
    lags[:, seq_len:] = jnp.zeros((rows, rows), F32)
    parts = [lags[a * 8 : (a + 1) * 8, :] for a in range(rows // 8)]
    shift = 8
    while len(parts) > 1:
        parts = [
            parts[a] + pltpu.roll(parts[a + 1], width - shift, 1) for a in range(0, len(parts), 2)
        ]
        shift *= 2
    skew = parts[0]
    row = iota((8, width), 0)
    for bit in (1, 2, 4):
        skew = jnp.where(row & bit != 0, pltpu.roll(skew, width - bit, 1), skew)
    corr = jnp.sum(skew, axis=0, keepdims=True)
    for i in range(ctx_size):
        lag_rows[i : i + 1, :] = corr[:, i * rows : (i + 1) * rows]
    term_send[...] = lag_rows[...].astype(BF16)

    @pl.when(core == 1)
    def _():
        pl.semaphore_wait(levels_ready, 1)

    def to_column(src, dst, phase):
        over_column(
            lambda target: push(
                src, dst, phase, {"dp": target["dp"], "ctx": ctx_index + 1 - core}
            )
        )

        @pl.when(core == 0)
        def _():
            push(src, dst, phase, mate)

    @pl.when(core == 1)
    def _():
        term_got[2 * level + 1] = term_send[...]

    to_column(term_send, term_got.at[2 * level + core], 1)

    modal = jnp.zeros((modes, rows), F32)
    direct = jnp.zeros((GROUP_SIZE, rows), F32)
    for i in range(ctx_size):
        span = slice(i * rows, (i + 1) * rows)
        modal = modal + basis[:, span] * corr[:, span]
        for s in range(PLANE_SEQS):
            direct = direct + got[s, i, :, :rows].astype(F32) * got[s, i, :, rows:].astype(F32)
    stack = jnp.concatenate(
        [modal, direct, jnp.zeros((rows - modes - GROUP_SIZE, rows), F32)], axis=0
    )
    small_send[...] = matmul(jnp.ones((8, rows), F32), stack, (1, 1), EXACT)[:1]

    @pl.when(core == 1)
    def _():
        small_got[2 * level + 1] = small_send[...]

    to_column(small_send, small_got.at[2 * level + core], 4)

    pairs = ctx_size // 2
    wide = [
        jnp.concatenate([got[s, 2 * p], got[s, 2 * p + 1]], axis=1)
        for p in range(pairs)
        for s in range(PLANE_SEQS)
    ]
    wide = jnp.concatenate(wide, axis=0)
    mix = jnp.concatenate([wide[:, :rows], wide[:, 2 * rows : 3 * rows]], axis=1)
    grad = jnp.concatenate([wide[:, rows : 2 * rows], wide[:, 3 * rows :]], axis=1)
    step = PLANE_SEQS * GROUP_SIZE
    state = jnp.zeros((pairs * step, 2 * rows), F32)
    prior = jnp.zeros((pairs * step, 2 * rows), F32)
    for q in range(pairs):
        block = jnp.concatenate(
            [
                taps[:, (2 * q + 1) * rows : (2 * q + 3) * rows],
                taps[:, 2 * q * rows : (2 * q + 2) * rows],
            ],
            axis=0,
        )
        cut = q * step
        ahead = matmul(mix[: pairs * step - cut], block)
        behind = matmul(grad[cut:], block, (1, 1))
        if q == 0:
            state, prior = ahead, behind
        else:
            gap = jnp.zeros((cut, 2 * rows), F32)
            state = state + jnp.concatenate([gap, ahead], axis=0)
            prior = prior + jnp.concatenate([behind, gap], axis=0)
    state = state.astype(BF16)
    prior = prior.astype(BF16)
    for s in range(PLANE_SEQS):
        for i in range(ctx_size):
            first_row = (i // 2) * step + s * GROUP_SIZE
            at = slice(first_row, first_row + GROUP_SIZE)
            span = slice((i % 2) * rows, (i % 2 + 1) * rows)
            back_send[s, i, :, :rows] = state[at, span]
            back_send[s, i, :, rows:] = prior[at, span]
    back_got[channels_of(plane_index)] = back_send[plane_seq, ctx_index]
    over_plane(
        lambda p, s, k, target: push(
            back_send.at[s, k], back_got.at[channels_of(plane_index)], 2, target
        )
    )

    filter_scale = 1.0 / math.sqrt(data_size * seq_len * GROUP_SIZE)
    at = iota((1, rows), 1)
    small_scale = jnp.where(
        at < modes, filter_scale / math.sqrt(seq_len), 1.0 / math.sqrt(data_size * seq_len)
    )
    pair = pl.ds(plane_index - 1, 2)

    @pl.when(core == 1)
    def _():
        arrived(term_got.at[pl.ds(0, 2 * depth - 1)], 1)
        arrived(small_got.at[pl.ds(0, 2 * depth - 1)], 4)
        for c in range(2):
            total = term_got[c].astype(F32)
            small = small_got[c]
            for i in range(1, depth):
                total = total + term_got[2 * i + c].astype(F32)
                small = small + small_got[2 * i + c]
            total = total * filter_scale
            small = small * small_scale
            for i in range(ctx_size):
                sum_send[i, c, :, :rows] = total[i : i + 1]
                sum_send[i, c, :, rows:] = small
        sum_got[pair] = sum_send[ctx_index]

        def push_sums(phase):
            return lambda p, s, k, target: push(
                sum_send.at[k], sum_got.at[pair], phase, target
            )

        over_chips(push_sums(3), 1, groups // 2 - 1)
        over_chips(push_sums(5), 0, groups // 2)

    arrived_plane(2)
    results = matmul(unsort[...], back_got[...])
    wide_gate = gate_out[...].astype(F32)
    wide_cot = cotangent[...].astype(F32)
    wide_in = gate_in[...].astype(F32)
    wide_signal = signal[...].astype(F32)
    mixed_wide = (wide_in * wide_signal).astype(BF16).astype(F32)
    back_wide = (wide_cot * wide_gate).astype(BF16).astype(F32)
    mixture = results[:, :rows] + bias_wide[...] * mixed_wide
    conv_out[...] = (wide_gate * mixture).astype(BF16)
    grad_gate_out[...] = (wide_cot * mixture).astype(BF16)
    grad_mixed = results[:, rows:] + bias_wide[...] * back_wide
    grad_gate_in[...] = (grad_mixed * wide_signal).astype(BF16)
    grad_signal[...] = (grad_mixed * wide_in).astype(BF16)

    @pl.when(core == 0)
    def _():
        arrived(sum_got, 5)

    @pl.when(core == 1)
    def _():
        arrived(sum_got.at[pl.ds(0, groups - 2)], 3)

    for g in range(groups):
        final[g : g + 1, :] = sum_got[g]
    grad_filter[...] = final[:, :rows]
    small = jnp.transpose(final[:, rows:])
    grad_residue[...] = small[:modes]
    terms = small[modes : modes + GROUP_SIZE]
    upper = terms.astype(BF16)
    middle = (terms - upper.astype(F32)).astype(BF16)
    lower = (terms - upper.astype(F32) - middle.astype(F32)).astype(BF16)
    spread = matmul(
        jnp.concatenate([upper, middle, lower], axis=0), jnp.where(member, 1.0, 0.0).astype(BF16)
    )
    spread = (
        spread[:GROUP_SIZE] + spread[GROUP_SIZE : 2 * GROUP_SIZE] + spread[2 * GROUP_SIZE :]
    )
    hit = iota((GROUP_SIZE, channels), 0).astype(F32) == ranks[...]
    grad_bias[...] = jnp.sum(jnp.where(hit, spread, 0.0), axis=0, keepdims=True)

    sent(sorted_in.at[pl.ds(0, channels - GROUP_SIZE)], 0)
    sent(back_got.at[pl.ds(0, channels - GROUP_SIZE)], 2)

    @pl.when(core == 0)
    def _():
        sent(term_got.at[pl.ds(0, depth)], 1)
        sent(small_got.at[pl.ds(0, depth)], 4)

    @pl.when(core == 1)
    def _():
        sent(term_got.at[pl.ds(0, depth - 1)], 1)
        sent(small_got.at[pl.ds(0, depth - 1)], 4)
        sent(sum_send.at[pl.ds(0, groups // 2 - 1)], 3)
        sent(sum_send, 5)


def store_kernel(count, *refs):
    sources, results, sems = refs[:count], refs[count : 2 * count], refs[2 * count]
    stores = [
        pltpu.make_async_copy(src, dst, sems.at[i])
        for i, (src, dst) in enumerate(zip(sources, results))
    ]
    for store in stores:
        store.start()
    for store in stores:
        store.wait()


def body(gate_out, gate_in, signal, cotangent, residue, decay, skip_bias, channel_group):
    data_size = lax.axis_size("dp")
    ctx_size = lax.axis_size("ctx")
    _, channels, rows = gate_out.shape
    groups, modes = residue.shape
    depth = data_size // PLANE_SEQS
    seq_len = rows * ctx_size
    vmem = pl.BlockSpec(memory_space=pltpu.VMEM)
    hbm = pl.BlockSpec(memory_space=pltpu.HBM)
    wide = jax.ShapeDtypeStruct((channels, rows), BF16)
    flat = lambda a: a.reshape(channels, rows)
    shapes = [
        wide,
        wide,
        wide,
        wide,
        jax.ShapeDtypeStruct((groups, rows), F32),
        jax.ShapeDtypeStruct((modes, groups), F32),
        jax.ShapeDtypeStruct((1, channels), F32),
    ]
    results = pl.pallas_call(
        functools.partial(kernel, data_size, ctx_size),
        out_shape=[pltpu.VMEM(a.shape, a.dtype) for a in shapes],
        in_specs=[hbm] * 8,
        out_specs=[vmem] * len(shapes),
        scratch_shapes=[
            pltpu.VMEM((channels, rows), BF16),
            pltpu.VMEM((channels, rows), BF16),
            pltpu.VMEM((channels, rows), BF16),
            pltpu.VMEM((channels, rows), BF16),
            pltpu.VMEM((modes, groups), F32),
            pltpu.VMEM((modes, groups), F32),
            pltpu.VMEM((1, channels), F32),
            pltpu.VMEM((1, channels), jnp.int32),
            pltpu.SemaphoreType.DMA((8,)),
            pltpu.VMEM((channels, 2 * rows), BF16),
            pltpu.VMEM((PLANE_SEQS, ctx_size, GROUP_SIZE, 2 * rows), BF16),
            pltpu.VMEM((channels, channels), BF16),
            pltpu.VMEM((channels, rows), F32),
            pltpu.VMEM((1, channels), F32),
            pltpu.VMEM((modes, seq_len), F32),
            pltpu.VMEM((rows, seq_len + rows), BF16),
            pltpu.VMEM((rows, seq_len + rows), F32),
            pltpu.VMEM((ctx_size, rows), F32),
            pltpu.VMEM((ctx_size, rows), BF16),
            pltpu.VMEM((2 * depth, ctx_size, rows), BF16),
            pltpu.VMEM((1, rows), F32),
            pltpu.VMEM((2 * depth, 1, rows), F32),
            pltpu.VMEM((PLANE_SEQS, ctx_size, GROUP_SIZE, 2 * rows), BF16),
            pltpu.VMEM((channels, 2 * rows), BF16),
            pltpu.VMEM((ctx_size, 2, 1, 2 * rows), F32),
            pltpu.VMEM((groups, 1, 2 * rows), F32),
            pltpu.VMEM((groups, 2 * rows), F32),
            pltpu.SemaphoreType.DMA((6,)),
            pltpu.SemaphoreType.DMA((6,)),
            pltpu.SemaphoreType.REGULAR,
            pltpu.SemaphoreType.REGULAR,
        ],
        compiler_params=pltpu.CompilerParams(
            collective_id=0, has_side_effects=True, vmem_limit_bytes=32 * 1024 * 1024
        ),
        cost_estimate=pl.CostEstimate(
            flops=2 * 400_000_000, bytes_accessed=2_000_000, transcendentals=100_000
        ),
    )(*[
        pltpu.with_memory_space_constraint(a, pltpu.HBM)
        for a in (
            flat(gate_out),
            flat(gate_in),
            flat(signal),
            flat(cotangent),
            residue.T,
            decay.T,
            skip_bias.reshape(1, channels),
            channel_group.reshape(1, channels),
        )
    ])
    results = pl.pallas_call(
        functools.partial(store_kernel, len(shapes)),
        out_shape=shapes,
        in_specs=[vmem] * len(shapes),
        out_specs=[hbm] * len(shapes),
        scratch_shapes=[pltpu.SemaphoreType.DMA((len(shapes),))],
        compiler_params=pltpu.CompilerParams(vmem_limit_bytes=4 * 1024 * 1024),
    )(*results)
    lifted = tuple(a.reshape(1, channels, rows) for a in results[:4])
    return lifted + (results[4], results[5].T, results[6].reshape(channels))


def solution(mesh):
    return jax.shard_map(
        body,
        mesh=mesh,
        in_specs=(
            P("dp", None, "ctx"),
            P("dp", None, "ctx"),
            P("dp", None, "ctx"),
            P("dp", None, "ctx"),
            P(),
            P(),
            P(),
            P(),
        ),
        out_specs=(
            P("dp", None, "ctx"),
            P("dp", None, "ctx"),
            P("dp", None, "ctx"),
            P("dp", None, "ctx"),
            P(None, "ctx"),
            P(),
            P(),
        ),
        check_vma=False,
    )
```

```python
import functools
import math

import jax
import jax.numpy as jnp
from jax import lax
from jax.experimental import pallas as pl
from jax.experimental.pallas import tpu as pltpu
from jax.sharding import PartitionSpec as P

GROUP_SIZE = 16
PLANE_SEQS = 2
MESH = pl.DeviceIdType.MESH
EXACT = lax.Precision.HIGHEST
F32 = jnp.float32
BF16 = jnp.bfloat16


def iota(shape, dim):
    return lax.broadcasted_iota(jnp.int32, shape, dim)


def matmul(left, right, dims=(1, 0), precision=None):
    return lax.dot_general(
        left,
        right,
        (((dims[0],), (dims[1],)), ((), ())),
        precision=precision,
        preferred_element_type=F32,
    )


def kernel(
    data_size,
    ctx_size,
    gate_out_hbm,
    gate_in_hbm,
    signal_hbm,
    cotangent_hbm,
    residue_hbm,
    decay_hbm,
    skip_bias_hbm,
    channel_group_hbm,
    conv_out,
    grad_gate_out,
    grad_gate_in,
    grad_signal,
    grad_filter,
    grad_residue,
    grad_bias,
    gate_out,
    gate_in,
    signal,
    cotangent,
    residue,
    decay,
    skip_bias,
    channel_group,
    load_sems,
    sorted_in,
    got,
    unsort,
    bias_wide,
    ranks,
    basis,
    taps,
    lags,
    lag_rows,
    term_send,
    term_got,
    small_send,
    small_got,
    back_send,
    back_got,
    sum_send,
    sum_got,
    final,
    send_sems,
    recv_sems,
    plane_ready,
    levels_ready,
):
    modes, groups = residue.shape
    channels, rows = gate_out.shape
    seq_len = rows * ctx_size
    depth = data_size // PLANE_SEQS
    blocks = ctx_size * GROUP_SIZE
    ctx_index = lax.axis_index("ctx")
    plane_seq = lax.axis_index("dp") // depth
    level = lax.axis_index("dp") % depth
    plane_index = plane_seq * ctx_size + ctx_index

    wide_y = ctx_size // 4
    core = lax.rem(ctx_index, 2)
    here_y = ctx_index // 4
    here_x = 2 * (lax.rem(ctx_index, 4) // 2) + plane_seq
    chips = []
    for dy in (2, 1, 3, 0)[4 - wide_y :]:
        y = lax.rem(here_y + dy, wide_y)
        for dx in (2, 1, 3, 0):
            x = lax.rem(here_x + dx, 4)
            seq = lax.rem(x, 2)
            chips.append((4 * y + x - seq, seq, seq * depth + level))
    half = depth // 2
    column = [half + (i + 1) // 2 * (1 - 2 * (i % 2)) for i in range(depth - 1)]
    column = [plane_seq * depth + lax.rem(level + o, depth) for o in column]

    def visit(step, chip, side):
        first, seq, data_rank = chip
        rank = first + side
        step(seq * ctx_size + rank, seq, rank, {"dp": data_rank, "ctx": rank})

    def over_plane(step):
        for chip in chips[:-1]:
            visit(step, chip, 1 - core)
            visit(step, chip, core)
        visit(step, chips[-1], 1 - core)

    def over_chips(step, side, count):
        for chip in chips[:count]:
            visit(step, chip, side)

    def over_column(step):
        for data_rank in column:
            step({"dp": data_rank})

    def push(src, dst, phase, target):
        pltpu.make_async_remote_copy(
            src_ref=src,
            dst_ref=dst,
            send_sem=send_sems.at[phase],
            recv_sem=recv_sems.at[phase],
            device_id=target,
            device_id_type=MESH,
        ).start()

    def arrived(span, phase):
        pltpu.make_async_copy(span, span, recv_sems.at[phase]).wait()

    def sent(span, phase):
        pltpu.make_async_copy(span, span, send_sems.at[phase]).wait()

    def arrived_plane(phase):
        span = sorted_in.at[pl.ds(0, channels - GROUP_SIZE)]
        arrived(span, phase)

    loads = [
        pltpu.make_async_copy(src, dst, load_sems.at[i])
        for i, (src, dst) in enumerate(
            [
                (channel_group_hbm, channel_group),
                (gate_in_hbm, gate_in),
                (signal_hbm, signal),
                (gate_out_hbm, gate_out),
                (cotangent_hbm, cotangent),
                (decay_hbm, decay),
                (residue_hbm, residue),
                (skip_bias_hbm, skip_bias),
            ]
        )
    ]
    for load in loads:
        load.start()

    barrier = pltpu.get_barrier_semaphore()
    mate = {"ctx": ctx_index + 1 - 2 * core}
    proxy_rank = ctx_index - lax.rem(ctx_index, 4) + 2
    on_proxy_chip = jnp.logical_and(plane_seq == 0, lax.rem(ctx_index, 4) >= 2)
    is_proxy = jnp.logical_and(on_proxy_chip, core == 0)
    row_size = 4 * PLANE_SEQS

    def greet(p, s, k, target):
        pl.semaphore_signal(barrier, inc=1, device_id=target, device_id_type=MESH)

    def greet_even(p, s, k, target):
        @pl.when(jnp.logical_or(s != 0, lax.rem(k, 4) != 2))
        def _():
            greet(p, s, k, target)

    for chip in chips[:-1]:
        visit(greet, chip, 1)
        visit(greet_even, chip, 0)

    @pl.when(jnp.logical_not(jnp.logical_and(on_proxy_chip, core == 1)))
    def _():
        pl.semaphore_signal(barrier, inc=1, device_id=mate, device_id_type=MESH)

    for data_rank in column:
        pl.semaphore_signal(
            barrier,
            inc=1,
            device_id={"dp": data_rank - plane_seq * depth, "ctx": proxy_rank},
            device_id_type=MESH,
        )

    loads[0].wait()
    member = iota((groups, channels), 0) == channel_group[...]
    before = jnp.where(iota((channels, channels), 0) < iota((channels, channels), 1), 1.0, 0.0)
    rank = matmul(jnp.where(member, 1.0, 0.0).astype(BF16), before.astype(BF16))
    rank = jnp.sum(jnp.where(member, rank, 0.0), axis=0, keepdims=True)
    ranks[...] = rank
    first = jnp.sum(
        jnp.where(member, iota((groups, channels), 0).astype(F32), 0.0), axis=0, keepdims=True
    )
    place = first * GROUP_SIZE + rank
    sort = jnp.where(iota((channels, channels), 0).astype(F32) == place, 1.0, 0.0).astype(BF16)

    for load in loads[1:5]:
        load.wait()
    mixed = (gate_in[...].astype(F32) * signal[...].astype(F32)).astype(BF16)
    back = (cotangent[...].astype(F32) * gate_out[...].astype(F32)).astype(BF16)
    sorted_in[...] = matmul(sort, jnp.concatenate([mixed, back], axis=1)).astype(BF16)

    def channels_of(peer):
        return pl.ds(pl.multiple_of(peer * GROUP_SIZE, GROUP_SIZE), GROUP_SIZE)

    got[plane_seq, ctx_index] = sorted_in[channels_of(plane_index)]

    @pl.when(jnp.logical_not(is_proxy))
    def _():
        pl.semaphore_wait(barrier, groups - 1)

    @pl.when(jnp.logical_and(on_proxy_chip, core == 1))
    def _():
        pl.semaphore_signal(plane_ready, inc=1, device_id=mate, device_id_type=MESH)

    @pl.when(is_proxy)
    def _():
        pl.semaphore_wait(plane_ready, 1)

    over_plane(
        lambda p, s, k, target: push(
            sorted_in.at[channels_of(p)], got.at[plane_seq, ctx_index], 0, target
        )
    )

    for load in loads[5:]:
        load.wait()
    place_wide = jnp.transpose(jnp.broadcast_to(place, (128, channels)))
    unsort[...] = jnp.where(
        iota((channels, channels), 1).astype(F32) == place_wide[:, :1], 1.0, 0.0
    ).astype(BF16)
    bias_wide[...] = jnp.transpose(jnp.broadcast_to(skip_bias[...], (rows, channels)))
    lane = iota((modes, rows), 1).astype(F32)
    pick = jnp.where(iota((groups, rows), 0) == plane_index, 1.0, 0.0)
    rate = matmul(decay[...], pick, precision=EXACT)
    weight = matmul(residue[...], pick, precision=EXACT)
    for i in range(ctx_size):
        basis[:, i * rows : (i + 1) * rows] = jnp.exp(-rate * ((lane + i * rows) / seq_len))
    filt = matmul(weight * jnp.exp(rate * (lane / seq_len)), basis[...], (0, 0), EXACT)
    causal = iota((rows, rows), 1) >= iota((rows, rows), 0)
    taps[:, :rows] = jnp.zeros((rows, rows), BF16)
    taps[:, rows : 2 * rows] = jnp.where(causal, filt[:, :rows], 0.0).astype(BF16)
    taps[:, 2 * rows :] = filt[:, rows:].astype(BF16)

    @pl.when(is_proxy)
    def _():
        pl.semaphore_wait(barrier, row_size * (depth - 1))

        def tell(i, c):
            seq = i // 4
            pl.semaphore_signal(
                levels_ready,
                inc=1,
                device_id={"dp": seq * depth + level, "ctx": proxy_rank - 2 + lax.rem(i, 4)},
                device_id_type=MESH,
            )
            return c

        lax.fori_loop(0, 2, tell, 0)
        lax.fori_loop(3, row_size, tell, 0)

    arrived_plane(0)

    mixes = [got[s, :, :, :rows].reshape(blocks, rows) for s in range(PLANE_SEQS)]
    grads = [got[s, :, :, rows:].reshape(blocks, rows) for s in range(PLANE_SEQS)]
    mix_t = jnp.transpose(jnp.concatenate(mixes, axis=0))

    def shifted(k):
        if k == 0:
            return jnp.concatenate(grads, axis=0)
        gap = jnp.zeros((k * GROUP_SIZE, rows), BF16)
        return jnp.concatenate([x for a in grads for x in (a[k * GROUP_SIZE :], gap)], axis=0)

    for k in range(0, ctx_size, 2):
        pair = jnp.concatenate([shifted(k), shifted(k + 1)], axis=1)
        lags[:, k * rows : (k + 2) * rows] = matmul(mix_t, pair)
    width = seq_len + rows
    lags[:, seq_len:] = jnp.zeros((rows, rows), F32)
    parts = [lags[a * 8 : (a + 1) * 8, :] for a in range(rows // 8)]
    shift = 8
    while len(parts) > 1:
        parts = [
            parts[a] + pltpu.roll(parts[a + 1], width - shift, 1) for a in range(0, len(parts), 2)
        ]
        shift *= 2
    skew = parts[0]
    row = iota((8, width), 0)
    for bit in (1, 2, 4):
        skew = jnp.where(row & bit != 0, pltpu.roll(skew, width - bit, 1), skew)
    corr = jnp.sum(skew, axis=0, keepdims=True)
    for i in range(ctx_size):
        lag_rows[i : i + 1, :] = corr[:, i * rows : (i + 1) * rows]
    term_send[...] = lag_rows[...].astype(BF16)

    @pl.when(jnp.logical_not(is_proxy))
    def _():
        pl.semaphore_wait(levels_ready, 1)

    def to_column(src, dst, phase):
        over_column(
            lambda target: push(
                src, dst, phase, {"dp": target["dp"], "ctx": ctx_index + 1 - core}
            )
        )

        @pl.when(core == 0)
        def _():
            push(src, dst, phase, mate)

    @pl.when(core == 1)
    def _():
        term_got[2 * level + 1] = term_send[...]

    to_column(term_send, term_got.at[2 * level + core], 1)

    modal = jnp.zeros((modes, rows), F32)
    direct = jnp.zeros((GROUP_SIZE, rows), F32)
    for i in range(ctx_size):
        span = slice(i * rows, (i + 1) * rows)
        modal = modal + basis[:, span] * corr[:, span]
        for s in range(PLANE_SEQS):
            direct = direct + got[s, i, :, :rows].astype(F32) * got[s, i, :, rows:].astype(F32)
    stack = jnp.concatenate(
        [modal, direct, jnp.zeros((rows - modes - GROUP_SIZE, rows), F32)], axis=0
    )
    small_send[...] = matmul(jnp.ones((8, rows), F32), stack, (1, 1), EXACT)[:1]

    @pl.when(core == 1)
    def _():
        small_got[2 * level + 1] = small_send[...]

    to_column(small_send, small_got.at[2 * level + core], 4)

    pairs = ctx_size // 2
    wide = [
        jnp.concatenate([got[s, 2 * p], got[s, 2 * p + 1]], axis=1)
        for p in range(pairs)
        for s in range(PLANE_SEQS)
    ]
    wide = jnp.concatenate(wide, axis=0)
    mix = jnp.concatenate([wide[:, :rows], wide[:, 2 * rows : 3 * rows]], axis=1)
    grad = jnp.concatenate([wide[:, rows : 2 * rows], wide[:, 3 * rows :]], axis=1)
    step = PLANE_SEQS * GROUP_SIZE
    state = jnp.zeros((pairs * step, 2 * rows), F32)
    prior = jnp.zeros((pairs * step, 2 * rows), F32)
    for q in range(pairs):
        block = jnp.concatenate(
            [
                taps[:, (2 * q + 1) * rows : (2 * q + 3) * rows],
                taps[:, 2 * q * rows : (2 * q + 2) * rows],
            ],
            axis=0,
        )
        cut = q * step
        ahead = matmul(mix[: pairs * step - cut], block)
        behind = matmul(grad[cut:], block, (1, 1))
        if q == 0:
            state, prior = ahead, behind
        else:
            gap = jnp.zeros((cut, 2 * rows), F32)
            state = state + jnp.concatenate([gap, ahead], axis=0)
            prior = prior + jnp.concatenate([behind, gap], axis=0)
    state = state.astype(BF16)
    prior = prior.astype(BF16)
    for s in range(PLANE_SEQS):
        for i in range(ctx_size):
            first_row = (i // 2) * step + s * GROUP_SIZE
            at = slice(first_row, first_row + GROUP_SIZE)
            span = slice((i % 2) * rows, (i % 2 + 1) * rows)
            back_send[s, i, :, :rows] = state[at, span]
            back_send[s, i, :, rows:] = prior[at, span]
    back_got[channels_of(plane_index)] = back_send[plane_seq, ctx_index]
    over_plane(
        lambda p, s, k, target: push(
            back_send.at[s, k], back_got.at[channels_of(plane_index)], 2, target
        )
    )

    filter_scale = 1.0 / math.sqrt(data_size * seq_len * GROUP_SIZE)
    at = iota((1, rows), 1)
    small_scale = jnp.where(
        at < modes, filter_scale / math.sqrt(seq_len), 1.0 / math.sqrt(data_size * seq_len)
    )
    pair = pl.ds(plane_index - 1, 2)

    @pl.when(core == 1)
    def _():
        arrived(term_got.at[pl.ds(0, 2 * depth - 1)], 1)
        arrived(small_got.at[pl.ds(0, 2 * depth - 1)], 4)
        for c in range(2):
            total = term_got[c].astype(F32)
            small = small_got[c]
            for i in range(1, depth):
                total = total + term_got[2 * i + c].astype(F32)
                small = small + small_got[2 * i + c]
            total = total * filter_scale
            small = small * small_scale
            for i in range(ctx_size):
                sum_send[i, c, :, :rows] = total[i : i + 1]
                sum_send[i, c, :, rows:] = small
        sum_got[pair] = sum_send[ctx_index]

        def push_sums(phase):
            return lambda p, s, k, target: push(
                sum_send.at[k], sum_got.at[pair], phase, target
            )

        over_chips(push_sums(3), 1, groups // 2 - 1)
        over_chips(push_sums(5), 0, groups // 2)

    arrived_plane(2)
    results = matmul(unsort[...], back_got[...])
    wide_gate = gate_out[...].astype(F32)
    wide_cot = cotangent[...].astype(F32)
    wide_in = gate_in[...].astype(F32)
    wide_signal = signal[...].astype(F32)
    mixed_wide = (wide_in * wide_signal).astype(BF16).astype(F32)
    back_wide = (wide_cot * wide_gate).astype(BF16).astype(F32)
    mixture = results[:, :rows] + bias_wide[...] * mixed_wide
    conv_out[...] = (wide_gate * mixture).astype(BF16)
    grad_gate_out[...] = (wide_cot * mixture).astype(BF16)
    grad_mixed = results[:, rows:] + bias_wide[...] * back_wide
    grad_gate_in[...] = (grad_mixed * wide_signal).astype(BF16)
    grad_signal[...] = (grad_mixed * wide_in).astype(BF16)

    @pl.when(core == 0)
    def _():
        arrived(sum_got, 5)

    @pl.when(core == 1)
    def _():
        arrived(sum_got.at[pl.ds(0, groups - 2)], 3)

    for g in range(groups):
        final[g : g + 1, :] = sum_got[g]
    grad_filter[...] = final[:, :rows]
    small = jnp.transpose(final[:, rows:])
    grad_residue[...] = small[:modes]
    terms = small[modes : modes + GROUP_SIZE]
    upper = terms.astype(BF16)
    middle = (terms - upper.astype(F32)).astype(BF16)
    lower = (terms - upper.astype(F32) - middle.astype(F32)).astype(BF16)
    spread = matmul(
        jnp.concatenate([upper, middle, lower], axis=0), jnp.where(member, 1.0, 0.0).astype(BF16)
    )
    spread = (
        spread[:GROUP_SIZE] + spread[GROUP_SIZE : 2 * GROUP_SIZE] + spread[2 * GROUP_SIZE :]
    )
    hit = iota((GROUP_SIZE, channels), 0).astype(F32) == ranks[...]
    grad_bias[...] = jnp.sum(jnp.where(hit, spread, 0.0), axis=0, keepdims=True)

    sent(sorted_in.at[pl.ds(0, channels - GROUP_SIZE)], 0)
    sent(back_got.at[pl.ds(0, channels - GROUP_SIZE)], 2)

    @pl.when(core == 0)
    def _():
        sent(term_got.at[pl.ds(0, depth)], 1)
        sent(small_got.at[pl.ds(0, depth)], 4)

    @pl.when(core == 1)
    def _():
        sent(term_got.at[pl.ds(0, depth - 1)], 1)
        sent(small_got.at[pl.ds(0, depth - 1)], 4)
        sent(sum_send.at[pl.ds(0, groups // 2 - 1)], 3)
        sent(sum_send, 5)


def store_kernel(count, *refs):
    sources, results, sems = refs[:count], refs[count : 2 * count], refs[2 * count]
    stores = [
        pltpu.make_async_copy(src, dst, sems.at[i])
        for i, (src, dst) in enumerate(zip(sources, results))
    ]
    for store in stores:
        store.start()
    for store in stores:
        store.wait()


def body(gate_out, gate_in, signal, cotangent, residue, decay, skip_bias, channel_group):
    data_size = lax.axis_size("dp")
    ctx_size = lax.axis_size("ctx")
    _, channels, rows = gate_out.shape
    groups, modes = residue.shape
    depth = data_size // PLANE_SEQS
    seq_len = rows * ctx_size
    vmem = pl.BlockSpec(memory_space=pltpu.VMEM)
    hbm = pl.BlockSpec(memory_space=pltpu.HBM)
    wide = jax.ShapeDtypeStruct((channels, rows), BF16)
    flat = lambda a: a.reshape(channels, rows)
    shapes = [
        wide,
        wide,
        wide,
        wide,
        jax.ShapeDtypeStruct((groups, rows), F32),
        jax.ShapeDtypeStruct((modes, groups), F32),
        jax.ShapeDtypeStruct((1, channels), F32),
    ]
    results = pl.pallas_call(
        functools.partial(kernel, data_size, ctx_size),
        out_shape=[pltpu.VMEM(a.shape, a.dtype) for a in shapes],
        in_specs=[hbm] * 8,
        out_specs=[vmem] * len(shapes),
        scratch_shapes=[
            pltpu.VMEM((channels, rows), BF16),
            pltpu.VMEM((channels, rows), BF16),
            pltpu.VMEM((channels, rows), BF16),
            pltpu.VMEM((channels, rows), BF16),
            pltpu.VMEM((modes, groups), F32),
            pltpu.VMEM((modes, groups), F32),
            pltpu.VMEM((1, channels), F32),
            pltpu.VMEM((1, channels), jnp.int32),
            pltpu.SemaphoreType.DMA((8,)),
            pltpu.VMEM((channels, 2 * rows), BF16),
            pltpu.VMEM((PLANE_SEQS, ctx_size, GROUP_SIZE, 2 * rows), BF16),
            pltpu.VMEM((channels, channels), BF16),
            pltpu.VMEM((channels, rows), F32),
            pltpu.VMEM((1, channels), F32),
            pltpu.VMEM((modes, seq_len), F32),
            pltpu.VMEM((rows, seq_len + rows), BF16),
            pltpu.VMEM((rows, seq_len + rows), F32),
            pltpu.VMEM((ctx_size, rows), F32),
            pltpu.VMEM((ctx_size, rows), BF16),
            pltpu.VMEM((2 * depth, ctx_size, rows), BF16),
            pltpu.VMEM((1, rows), F32),
            pltpu.VMEM((2 * depth, 1, rows), F32),
            pltpu.VMEM((PLANE_SEQS, ctx_size, GROUP_SIZE, 2 * rows), BF16),
            pltpu.VMEM((channels, 2 * rows), BF16),
            pltpu.VMEM((ctx_size, 2, 1, 2 * rows), F32),
            pltpu.VMEM((groups, 1, 2 * rows), F32),
            pltpu.VMEM((groups, 2 * rows), F32),
            pltpu.SemaphoreType.DMA((6,)),
            pltpu.SemaphoreType.DMA((6,)),
            pltpu.SemaphoreType.REGULAR,
            pltpu.SemaphoreType.REGULAR,
        ],
        compiler_params=pltpu.CompilerParams(
            collective_id=0, has_side_effects=True, vmem_limit_bytes=32 * 1024 * 1024
        ),
        cost_estimate=pl.CostEstimate(
            flops=2 * 400_000_000, bytes_accessed=2_000_000, transcendentals=100_000
        ),
    )(*[
        pltpu.with_memory_space_constraint(a, pltpu.HBM)
        for a in (
            flat(gate_out),
            flat(gate_in),
            flat(signal),
            flat(cotangent),
            residue.T,
            decay.T,
            skip_bias.reshape(1, channels),
            channel_group.reshape(1, channels),
        )
    ])
    results = pl.pallas_call(
        functools.partial(store_kernel, len(shapes)),
        out_shape=shapes,
        in_specs=[vmem] * len(shapes),
        out_specs=[hbm] * len(shapes),
        scratch_shapes=[pltpu.SemaphoreType.DMA((len(shapes),))],
        compiler_params=pltpu.CompilerParams(vmem_limit_bytes=4 * 1024 * 1024),
    )(*results)
    lifted = tuple(a.reshape(1, channels, rows) for a in results[:4])
    return lifted + (results[4], results[5].T, results[6].reshape(channels))


def solution(mesh):
    return jax.shard_map(
        body,
        mesh=mesh,
        in_specs=(
            P("dp", None, "ctx"),
            P("dp", None, "ctx"),
            P("dp", None, "ctx"),
            P("dp", None, "ctx"),
            P(),
            P(),
            P(),
            P(),
        ),
        out_specs=(
            P("dp", None, "ctx"),
            P("dp", None, "ctx"),
            P("dp", None, "ctx"),
            P("dp", None, "ctx"),
            P(None, "ctx"),
            P(),
            P(),
        ),
        check_vma=False,
    )
```
